256 devices in a mesh: gz: 2 (over x_hi), row: 16 (over z, core), col: 8 (over x_lo, y).
Axes of the slice: x: 4 (x_hi: 2, x_lo: 2; x = x_hi * 2 + x_lo), y: 4, z: 8, core: 2. Of those that a mesh axis runs over, the one named last changes fastest.
Arguments:
- volume: bfloat16 [32, 1024, 2048], P('gz', 'row', 'col'), may hold values from -7 to 7
Outputs:
- tensor: float32 [6, 8, 256, 512], P(None, 'gz', 'row', 'col')
The draws below stay inside these ranges and needn't reach their ends.
All inputs are finite; a program needn't handle non-finite values.
Results may differ from the reference program's by a relative error of at most 0.0028.
Values may be sent and summed in bfloat16 or wider, within the bound.
A program may use at most 128 MiB of HBM per device.

```python
import math
import jax
import jax.numpy as jnp
from jax import lax

CX = 256
R = 3
R2 = 8
NZ = 32
NY = 1024
NX = 2048
N_COL = 8


def draw_volume(key, part):
    key = jax.random.fold_in(key, 11)
    key_family, key_azimuth, key_height, key_number, key_phase, key_noise = jax.random.split(key, 6)
    z_regions = NZ // 16
    y_regions = NY // 32
    x_regions = NX // 32
    region_shape = (z_regions, 1, y_regions, 1, x_regions, 1)
    family = jax.random.randint(key_family, region_shape, 0, 4)
    aligned = (family == 0).astype(jnp.float32)
    diagonal_low = (family == 1).astype(jnp.float32)
    diagonal_high = (family == 2).astype(jnp.float32)
    oblique = (family == 3).astype(jnp.float32)
    azimuth = jax.random.uniform(key_azimuth, region_shape, jnp.float32, -math.pi, math.pi)
    height = jax.random.uniform(key_height, region_shape, jnp.float32, -1.0, 1.0)
    radial = jnp.sqrt(jnp.maximum(1.0 - height * height, 0.0))
    number = jax.random.uniform(key_number, region_shape, jnp.float32, 0.5, 1.2)
    phases = jax.random.uniform(key_phase, region_shape, jnp.float32, -math.pi, math.pi)
    quarter = math.pi / 4.0
    halfway = math.pi / 2.0
    wave_z = quarter * diagonal_low + halfway * diagonal_high + oblique * number * height
    wave_y = quarter * diagonal_low + halfway * diagonal_high + oblique * number * radial * jnp.sin(azimuth)
    wave_x = halfway * aligned + quarter * diagonal_low + halfway * diagonal_high + oblique * number * radial * jnp.cos(azimuth)
    strength = 1.5 * aligned + 1.8 * diagonal_low + 5.5 * diagonal_high + 1.5 * oblique
    z_coord = jnp.arange(NZ).astype(jnp.float32).reshape(z_regions, 16, 1, 1, 1, 1)
    y_coord = jnp.arange(NY).astype(jnp.float32).reshape(1, 1, y_regions, 32, 1, 1)
    x_coord = jnp.arange(NX).astype(jnp.float32).reshape(1, 1, 1, 1, x_regions, 32)
    angles = wave_z * z_coord + wave_y * y_coord + wave_x * x_coord + phases
    full_shape = (z_regions, 16, y_regions, 32, x_regions, 32)
    noises = 0.3 * jnp.clip(jax.random.normal(key_noise, full_shape, jnp.float32), -3.0, 3.0)
    field_values = strength * jnp.cos(angles) + noises
    return field_values.reshape(NZ, NY, NX).astype(jnp.bfloat16)


def setup_inputs(seed: int = 0) -> dict:
    key_of = jax.random.split(jax.random.key(seed), 2)
    return {
        "volume": draw_volume(jax.random.fold_in(key_of[1], 71), 0),
    }


pair_table = ((0, 0), (1, 1), (2, 2), (0, 1), (0, 2), (1, 2))


def gauss_taps(radius):
    offsets = jnp.arange(-radius, radius + 1).astype(jnp.float32)
    spread = radius / 3.0
    smooth = jnp.exp(-offsets * offsets / (2.0 * spread * spread))
    smooth = smooth / jnp.sum(smooth)
    slopes = offsets * smooth
    slopes = slopes / jnp.sum(offsets * slopes)
    return smooth.astype(jnp.bfloat16), slopes.astype(jnp.bfloat16)


def pad_along(source, along_dim, radius):
    widths = [(0, 0)] * source.ndim
    widths[along_dim] = (radius, radius)
    return jnp.pad(source, widths)


def correlate(source, tap_values, along_dim, radius, stride, with_pad):
    padded = pad_along(source, along_dim, radius) if with_pad else source
    length = padded.shape[along_dim] - 2 * radius
    weights = tap_values.astype(jnp.float32)
    summed = jnp.zeros(lax.slice_in_dim(padded, 0, length, stride=stride, axis=along_dim).shape, jnp.float32)
    for offset in range(2 * radius + 1):
        shifted = lax.slice_in_dim(padded, offset, offset + length, stride=stride, axis=along_dim)
        summed = summed + weights[offset] * shifted.astype(jnp.float32)
    return summed


def reference(volume):
    smooth_d, slope_d = gauss_taps(R)
    smooth_i, unused = gauss_taps(R2)
    margin = R + R2
    padded = pad_along(volume, 2, margin)

    def one_strip(strip_index):
        start_col = strip_index * CX
        strip_cells = lax.dynamic_slice_in_dim(padded, start_col, CX + 2 * margin, 2)
        z_smooth = correlate(strip_cells, smooth_d, 0, R, 1, True).astype(jnp.bfloat16)
        z_slope = correlate(strip_cells, slope_d, 0, R, 1, True).astype(jnp.bfloat16)
        plane_gg = correlate(z_smooth, smooth_d, 1, R, 1, True).astype(jnp.bfloat16)
        plane_dg = correlate(z_smooth, slope_d, 1, R, 1, True).astype(jnp.bfloat16)
        plane_gd = correlate(z_slope, smooth_d, 1, R, 1, True).astype(jnp.bfloat16)
        grad_x = correlate(plane_gg, slope_d, 2, R, 1, False)
        grad_y = correlate(plane_dg, smooth_d, 2, R, 1, False)
        grad_z = correlate(plane_gd, smooth_d, 2, R, 1, False)
        gradients = [grad_x.astype(jnp.bfloat16), grad_y.astype(jnp.bfloat16), grad_z.astype(jnp.bfloat16)]
        columns = jnp.arange(CX + 2 * R2).astype(jnp.int32) + start_col - R2
        inside = ((columns >= 0) & (columns < NX)).astype(jnp.float32)
        outputs = []
        for first_pair, second_pair in pair_table:
            product = gradients[first_pair].astype(jnp.float32) * gradients[second_pair].astype(jnp.float32)
            product = (product * inside).astype(jnp.bfloat16)
            smooth_x = correlate(product, smooth_i, 2, R2, 4, False).astype(jnp.bfloat16)
            smooth_y = correlate(smooth_x, smooth_i, 1, R2, 4, True).astype(jnp.bfloat16)
            outputs.append(correlate(smooth_y, smooth_i, 0, R2, 4, True))
        return jnp.stack(outputs)

    strips = lax.map(one_strip, jnp.arange(N_COL, dtype=jnp.int32))
    return jnp.transpose(strips, (1, 2, 3, 0, 4)).reshape(6, NZ // 4, NY // 4, NX // 4)
```

```python
import itertools

import jax
import jax.numpy as jnp
import ml_dtypes
import numpy as np
from jax import lax
from jax.experimental import pallas as pl
from jax.experimental.pallas import tpu as pltpu
from jax.sharding import PartitionSpec as P

R = 3
R2 = 8
MARGIN = R + R2
BF16 = ml_dtypes.bfloat16
F32 = jnp.float32
MESH = pl.DeviceIdType.MESH

DZ, DY, DX = 16, 64, 256
WY, GY = DY + 32, DY + 2 * R2
QZ, QY, QX = DZ // 4, DY // 4, DX // 4
SLOT = 16
HALF = DZ // 2
NEIGHBOURS = tuple(o for o in itertools.product((0, 1), (-1, 0, 1), (-1, 0, 1)) if o != (0, 0, 0))
pair_table = ((0, 0), (1, 1), (2, 2), (0, 1), (0, 2), (1, 2))


def gauss_taps(radius):
    offsets = np.arange(-radius, radius + 1).astype(np.float32)
    spread = np.float32(radius / 3.0)
    smooth = np.exp(-offsets * offsets / (np.float32(2.0) * spread * spread))
    smooth = smooth / np.sum(smooth)
    slopes = offsets * smooth
    slopes = slopes / np.sum(offsets * slopes)
    return [t.astype(BF16).astype(np.float32) for t in (smooth, slopes)]


SMOOTH, SLOPE = gauss_taps(R)
WIDE, _ = gauss_taps(R2)


def banded(taps, radius, source, target):
    s = np.asarray(source)[:, None] - np.asarray(target)[None, :]
    picked = taps[np.clip(s + radius, 0, 2 * radius)]
    return np.where(np.abs(s) <= radius, picked, np.float32(0.0))


def layer_targets(gz):
    return [0, 4, 8, 12] + ([16, 20] if gz == 0 else [-8, -4])


def constants():
    y_in, y_out, y_coarse = np.arange(WY) - 16, np.arange(GY) - R2, 4 * np.arange(QY)
    x_all, x_coarse = np.arange(DX), 4 * np.arange(QX)
    ty = []
    for edge in range(3):
        inside = np.ones(GY, np.float32)
        if edge == 0:
            inside[y_out < 0] = 0
        if edge == 2:
            inside[y_out >= DY] = 0
        ty.append(np.concatenate([banded(t, R, y_in, y_out).T * inside[:, None] for t in (SMOOTH, SLOPE)]))
    x_pair = np.stack([banded(SLOPE, R, x_all, x_all), banded(SMOOTH, R, x_all, x_all)])
    ay = banded(WIDE, R2, y_out, y_coarse).T
    near, far = [], []
    for gz in range(2):
        targets = layer_targets(gz)
        near_z, far_z = HALF * (1 - gz) + np.arange(HALF), HALF * gz + np.arange(HALF)
        near.append(np.kron(banded(WIDE, R2, near_z, targets).T, ay))
        far.append(np.kron(banded(WIDE, R2, far_z, targets[:QZ]).T, ay))
    mx = np.zeros((DX, 128), np.float32)
    mx[:, :QX] = banded(WIDE, R2, x_all, x_coarse)
    mx[:R] = 0
    mx[DX - R :] = 0
    cols = np.arange(MARGIN)
    pad_in, pad_out = ((0, SLOT - MARGIN), (0, SLOT - MARGIN)), ((0, 0), (0, 0))
    wp = []
    for side_in, x_out, outside in (
        ((cols - MARGIN, cols), cols - R2, lambda x: x < 0),
        ((cols + DX - MARGIN, cols + DX), cols + DX - R, lambda x: x >= DX),
    ):
        for masked in (False, True):
            blocks = []
            for x_in in side_in:
                row = []
                for t in (SMOOTH, SLOPE):
                    w = banded(t, R, x_in, x_out)
                    if masked:
                        w = np.where(outside(x_out)[None, :], np.float32(0.0), w)
                    row.append(np.kron(np.eye(8, dtype=np.float32), np.pad(w, pad_in)))
                blocks.append(np.concatenate(row, axis=1))
            wp.append(np.concatenate(blocks, axis=0))
    wz, wzx = [], []
    one = np.eye(SLOT, dtype=np.float32)
    for gz in range(2):
        z_halo = DZ + np.arange(8) if gz == 0 else np.arange(8) - R
        rows = []
        for z_in, used in ((np.arange(DZ), DZ), (z_halo, R)):
            keep = (np.arange(len(z_in)) < used)[:, None]
            rows.append(
                np.concatenate(
                    [np.kron(banded(t, R, z_in, np.arange(DZ)) * keep, one) for t in (SMOOTH, SLOPE)], axis=1
                )
            )
        wz.append(np.concatenate(rows, axis=0))
        bz = banded(WIDE, R2, np.arange(DZ), layer_targets(gz))
        sides = []
        for x_out in (cols - R2, cols + DX - R):
            bx = np.zeros((SLOT, 128), np.float32)
            bx[:MARGIN, :QX] = banded(WIDE, R2, x_out, x_coarse)
            sides.append(np.kron(bz, bx))
        wzx.append(np.concatenate(sides, axis=0))
    stacks = (np.stack(ty), x_pair, np.stack(near), np.stack(far), mx, np.stack(wp), np.stack(wz), ay, np.stack(wzx))
    return [np.asarray(a, np.float32).astype(BF16) for a in stacks]


def mm(a, b):
    return jnp.dot(a, b, preferred_element_type=F32)


def kernel(
    n_row, n_col,
    vol, ty_h, xp_h, near_h, far_h, mx_h, wp_h, wz_h, ay_h, wzx_h,
    out,
    f, strips, strips_z, send_z, zs, zd, planes, grads, prods, acc, panel, xpanel, zpanel, gpanel, psend, precv,
    ty, xp, near, far, mx, wpl, wpr, wz, ay, wzx,
    local_sem, send_sem, recv_sem,
):
    gz, row, col = lax.axis_index("gz"), lax.axis_index("row"), lax.axis_index("col")
    has = {(1, -1): row > 0, (1, 1): row < n_row - 1, (2, -1): col > 0, (2, 1): col < n_col - 1}

    def exists(o):
        tests = [has[d, o[d]] for d in (1, 2) if o[d]]
        if not tests:
            return None
        return tests[0] if len(tests) == 1 else tests[0] & tests[1]

    def when(o, fn):
        ok = exists(o)
        if ok is None:
            fn()
        else:
            pl.when(ok)(fn)

    def peer(o):
        return (lax.rem(gz + o[0], 2), row + o[1], col + o[2])

    barrier = pltpu.get_barrier_semaphore()
    count = 0
    for o in NEIGHBOURS:
        when(o, lambda o=o: pl.semaphore_signal(barrier, inc=1, device_id=peer(o), device_id_type=MESH))
        ok = exists(o)
        count = count + (1 if ok is None else ok.astype(jnp.int32))

    own_z, own_y = pl.ds(R, DZ), pl.ds(16, DY)
    first_y, last_y, top_y, bottom_y = pl.ds(16, 16), pl.ds(DY, 16), pl.ds(0, 16), pl.ds(DY + 16, 16)
    load = pltpu.make_async_copy(vol, f.at[own_z, own_y], local_sem.at[0])
    load.start()
    edge = jnp.where(row == 0, 0, jnp.where(row == n_row - 1, 2, 1))
    fetches = [
        (ty_h.at[edge], ty), (xp_h, xp), (near_h.at[gz], near), (far_h.at[gz], far), (mx_h, mx),
        (wp_h.at[(col == 0).astype(jnp.int32)], wpl), (wp_h.at[2 + (col == n_col - 1).astype(jnp.int32)], wpr),
        (wz_h.at[gz], wz), (ay_h, ay), (wzx_h.at[gz], wzx),
    ]
    fetches = [pltpu.make_async_copy(s, d, local_sem.at[1 + i]) for i, (s, d) in enumerate(fetches)]
    for c in fetches:
        c.start()

    dead_z = pl.ds((R + DZ) * gz, R)
    f[dead_z] = jnp.zeros((R, WY, DX), jnp.bfloat16)
    for d, where_y in ((-1, top_y), (1, bottom_y)):
        @pl.when(jnp.logical_not(has[1, d]))
        def _(where_y=where_y):
            f[:, where_y] = jnp.zeros((DZ + 2 * R, 16, DX), jnp.bfloat16)
            strips[:, where_y] = jnp.zeros((4, 16, 256), jnp.bfloat16)
            strips_z[:, where_y] = jnp.zeros((4, 16, 128), jnp.bfloat16)
    for d, kind in ((-1, 0), (1, 3)):
        @pl.when(jnp.logical_not(has[2, d]))
        def _(kind=kind):
            strips[kind] = jnp.zeros((WY, 256), jnp.bfloat16)
            strips_z[kind] = jnp.zeros((WY, 128), jnp.bfloat16)

    load.wait()
    near_z = 13 * (1 - gz)

    def pack(layers):
        lane = lax.broadcasted_iota(jnp.int32, (DY, 128), 1)
        first, last = (jnp.zeros((DY, 128), F32) for _ in range(2))
        for t, z in enumerate(layers):
            tile = f[R + z, 16 : 16 + DY, :]
            use = (lane >= SLOT * t) & (lane < SLOT * t + MARGIN)
            first = jnp.where(use, pltpu.roll(tile[:, :128].astype(F32), SLOT * t, 1), first)
            last = jnp.where(use, pltpu.roll(tile[:, 128:].astype(F32), (SLOT * t + MARGIN) % 128, 1), last)
        return first.astype(jnp.bfloat16), last.astype(jnp.bfloat16)

    for h in range(2):
        first, last = pack([HALF * h + t for t in range(8)])
        strips[1, 16 : 16 + DY, 128 * h : 128 * h + 128] = first
        strips[2, 16 : 16 + DY, 128 * h : 128 * h + 128] = last
    first, last = pack([near_z + t for t in range(R)])
    send_z[0] = first
    send_z[1] = last

    messages = []

    def message(o, source, target):
        i = len(messages)
        c = pltpu.make_async_remote_copy(
            src_ref=source, dst_ref=target, send_sem=send_sem.at[i], recv_sem=recv_sem.at[i],
            device_id=peer(o), device_id_type=MESH,
        )
        messages.append((o, c))

    near_layers, halo_layers = pl.ds(near_z, R), pl.ds((R + DZ) * gz, R)
    both = pl.ds(0, 2)
    own_kinds = pl.ds(1, 2)
    y_cut = {0: (pl.ds(0, DY), own_y), 1: (pl.ds(DY - 16, 16), top_y), -1: (pl.ds(0, 16), bottom_y)}
    for o in sorted(NEIGHBOURS, key=lambda o: -(2 * o[0] + abs(o[1]) + abs(o[2])) - 9 * (o == (1, 0, 0))):
        a, b, c = o
        src_y, dst_y = y_cut[b]
        strip_y = pl.ds(16 + (DY - 16 if b == 1 else 0), DY if b == 0 else 16)
        if c == 0 and a == 0:
            message(o, vol.at[:, src_y], f.at[own_z, dst_y])
            message(o, strips.at[own_kinds, strip_y], strips.at[own_kinds, dst_y])
        elif c == 0:
            message(o, vol.at[near_layers, src_y], f.at[halo_layers, dst_y])
            message(o, send_z.at[both, src_y], strips_z.at[own_kinds, dst_y])
        else:
            mine, theirs = (2, 0) if c == 1 else (1, 3)
            if a == 0:
                message(o, strips.at[mine, strip_y], strips.at[theirs, dst_y])
            else:
                message(o, send_z.at[mine - 1, src_y], strips_z.at[theirs, dst_y])

    pl.semaphore_wait(barrier, count)
    for o, c in messages:
        when(o, lambda c=c: c.start())
    for c in fetches:
        c.wait()
    for o, c in messages:
        when((o[0], -o[1], -o[2]), lambda c=c: c.wait_recv())

    def products(get, put):
        g = [get(i) for i in range(3)]
        for c, (i, j) in enumerate(pair_table):
            put(c, g[i] * g[j])

    for side, (k, w) in enumerate(((0, wpl), (2, wpr))):
        for t in range(3):
            src = [(strips[i, :, 128 * t : 128 * t + 128] if t < 2 else strips_z[i]) for i in (k, k + 1)]
            xs = mm(jnp.concatenate(src, axis=1), w[...]).astype(jnp.bfloat16)
            xpanel[0, :, 128 * t : 128 * t + 128] = xs[:, :128]
            xpanel[1, :, 128 * t : 128 * t + 128] = xs[:, 128:]
        zpanel[0] = mm(xpanel[1], wz[:, :256]).astype(jnp.bfloat16)
        zpanel[1] = mm(xpanel[0], wz[:, :256]).astype(jnp.bfloat16)
        zpanel[2] = mm(xpanel[0], wz[:, 256:]).astype(jnp.bfloat16)
        edge_grads = [
            mm(ty[:GY] if i != 1 else ty[GY:], zpanel[i]).astype(jnp.bfloat16) for i in range(3)
        ]

        def put(c, p, side=side):
            gpanel[16 * c : 16 * c + 16, 256 * side : 256 * side + 256] = mm(ay[...], p).astype(jnp.bfloat16)

        products(lambda i: edge_grads[i], put)
    panel[...] = mm(gpanel[...], wzx[...])

    def gradients(z_base):
        def four_layers(g, _):
            z0 = z_base + 4 * g
            for y in range(0, WY, 16):
                for x in range(0, DX, 128):
                    v = [f[z0 + i, y : y + 16, x : x + 128].astype(F32) for i in range(4 + 2 * R)]
                    for j in range(4):
                        c = v[j : j + 7]
                        smooth, slope = c[3] * float(SMOOTH[R]), None
                        for s in (1, 2, 3):
                            smooth = smooth + (c[3 - s] + c[3 + s]) * float(SMOOTH[R + s])
                            term = (c[3 + s] - c[3 - s]) * float(SLOPE[R + s])
                            slope = term if slope is None else slope + term
                        zs[j, y : y + 16, x : x + 128] = smooth.astype(jnp.bfloat16)
                        zd[j, y : y + 16, x : x + 128] = slope.astype(jnp.bfloat16)
            for j in range(4):
                pair = mm(ty[...], zs[j]).astype(jnp.bfloat16)
                at = slice(GY * j, GY * j + GY)
                planes[0, at] = pair[:GY]
                planes[1, at] = pair[GY:]
                planes[2, at] = mm(ty[:GY], zd[j]).astype(jnp.bfloat16)
            for i in range(3):
                grads[i] = mm(planes[i], xp[0 if i == 0 else 1]).astype(jnp.bfloat16)
            for y in range(0, 4 * GY, 16):
                at = pl.ds(pl.multiple_of(4 * GY * g, 16) + y, 16)

                def put(c, p, at=at):
                    prods[c, at] = p

                products(lambda i, y=y: grads[i, y : y + 16], put)
            return 0

        lax.fori_loop(0, 2, four_layers, 0)

    gradients(HALF * (1 - gz))
    for c in range(6):
        s = mm(near[...], prods[c])
        acc[c] = s[: QZ * QY]
        reach = mm(s[QZ * QY :].astype(jnp.bfloat16), mx[...])
        for q in range(2):
            edge_part = panel[16 * c : 16 * c + 16, 128 * (QZ + q) : 128 * (QZ + q) + 128]
            psend[c, 16 * q : 16 * q + 16] = (reach[16 * q : 16 * q + 16] + edge_part).astype(jnp.bfloat16)
    message((1, 0, 0), psend, precv)
    messages[-1][1].start()

    gradients(HALF * gz)
    for c in range(6):
        s = acc[c] + mm(far[...], prods[c])
        own = mm(s.astype(jnp.bfloat16), mx[...])
        for q in range(QZ):
            part = own[16 * q : 16 * q + 16] + panel[16 * c : 16 * c + 16, 128 * q : 128 * q + 128]
            out[c, q] = part[:, :QX]
    messages[-1][1].wait_recv()
    for q in range(2):
        for c in range(6):
            got = precv[c, 16 * q : 16 * q + 16, :QX].astype(F32)
            out[c, 2 * (1 - gz) + q] += got
    for o, c in messages:
        when(o, lambda c=c: c.wait_send())


def solution(mesh):
    n_row, n_col = mesh.shape["row"], mesh.shape["col"]
    consts = constants()
    bf = jnp.bfloat16
    hbm = pl.BlockSpec(memory_space=pltpu.HBM)

    def per_device(volume):
        return pl.pallas_call(
            lambda *refs: kernel(n_row, n_col, *refs),
            name="structure_tensor",
            out_shape=jax.ShapeDtypeStruct((6, QZ, QY, QX), F32),
            in_specs=[hbm] * (1 + len(consts)),
            out_specs=pl.BlockSpec(memory_space=pltpu.VMEM),
            scratch_shapes=[
                pltpu.VMEM((DZ + 2 * R, WY, DX), bf),
                pltpu.VMEM((4, WY, 256), bf),
                pltpu.VMEM((4, WY, 128), bf),
                pltpu.VMEM((2, DY, 128), bf),
                pltpu.VMEM((4, WY, DX), bf),
                pltpu.VMEM((4, WY, DX), bf),
                pltpu.VMEM((3, 4 * GY, DX), bf),
                pltpu.VMEM((3, 4 * GY, DX), bf),
                pltpu.VMEM((6, HALF * GY, DX), bf),
                pltpu.VMEM((6, QZ * QY, DX), F32),
                pltpu.VMEM((96, 768), F32),
                pltpu.VMEM((2, WY, 384), bf),
                pltpu.VMEM((3, WY, 256), bf),
                pltpu.VMEM((96, 512), bf),
                pltpu.VMEM((6, 32, 128), bf),
                pltpu.VMEM((6, 32, 128), bf),
                pltpu.VMEM((2 * GY, WY), bf),
                pltpu.VMEM((2, DX, DX), bf),
                pltpu.VMEM((6 * 16, HALF * GY), bf),
                pltpu.VMEM((4 * 16, HALF * GY), bf),
                pltpu.VMEM((DX, 128), bf),
                pltpu.VMEM((256, 256), bf),
                pltpu.VMEM((256, 256), bf),
                pltpu.VMEM((384, 512), bf),
                pltpu.VMEM((16, GY), bf),
                pltpu.VMEM((512, 768), bf),
                pltpu.SemaphoreType.DMA((11,)),
                pltpu.SemaphoreType.DMA((23,)),
                pltpu.SemaphoreType.DMA((23,)),
            ],
            compiler_params=pltpu.CompilerParams(
                collective_id=0, has_side_effects=True, vmem_limit_bytes=32 * 2**20
            ),
        )(volume, *[jnp.asarray(a) for a in consts])

    return jax.shard_map(
        per_device,
        mesh=mesh,
        in_specs=(P("gz", "row", "col"),),
        out_specs=P(None, "gz", "row", "col"),
        check_vma=False,
    )
```

```python
import itertools

import jax
import jax.numpy as jnp
import ml_dtypes
import numpy as np
from jax import lax
from jax.experimental import pallas as pl
from jax.experimental.pallas import tpu as pltpu
from jax.sharding import PartitionSpec as P

R = 3
R2 = 8
MARGIN = R + R2
BF16 = ml_dtypes.bfloat16
F32 = jnp.float32
MESH = pl.DeviceIdType.MESH

DZ, DY, DX = 16, 64, 256
WY, GY = DY + 32, DY + 2 * R2
QZ, QY, QX = DZ // 4, DY // 4, DX // 4
SLOT = 16
HALF = DZ // 2
VMEM_BYTES = 32 * 2**20
NEIGHBOURS = tuple(o for o in itertools.product((0, 1), (-1, 0, 1), (-1, 0, 1)) if o != (0, 0, 0))
pair_table = ((0, 0), (1, 1), (2, 2), (0, 1), (0, 2), (1, 2))


def gauss_taps(radius):
    offsets = np.arange(-radius, radius + 1).astype(np.float32)
    spread = np.float32(radius / 3.0)
    smooth = np.exp(-offsets * offsets / (np.float32(2.0) * spread * spread))
    smooth = smooth / np.sum(smooth)
    slopes = offsets * smooth
    slopes = slopes / np.sum(offsets * slopes)
    return [t.astype(BF16).astype(np.float32) for t in (smooth, slopes)]


SMOOTH, SLOPE = gauss_taps(R)
WIDE, _ = gauss_taps(R2)


def banded(taps, radius, source, target):
    s = np.asarray(source)[:, None] - np.asarray(target)[None, :]
    picked = taps[np.clip(s + radius, 0, 2 * radius)]
    return np.where(np.abs(s) <= radius, picked, np.float32(0.0))


def layer_targets(gz):
    return [0, 4, 8, 12] + ([16, 20] if gz == 0 else [-8, -4])


def constants():
    y_in, y_out, y_coarse = np.arange(WY) - 16, np.arange(GY) - R2, 4 * np.arange(QY)
    x_all, x_coarse = np.arange(DX), 4 * np.arange(QX)
    ty = []
    for edge in range(3):
        inside = np.ones(GY, np.float32)
        if edge == 0:
            inside[y_out < 0] = 0
        if edge == 2:
            inside[y_out >= DY] = 0
        ty.append(np.concatenate([banded(t, R, y_in, y_out).T * inside[:, None] for t in (SMOOTH, SLOPE)]))
    x_pair = np.stack([banded(SLOPE, R, x_all, x_all), banded(SMOOTH, R, x_all, x_all)])
    ay = banded(WIDE, R2, y_out, y_coarse).T
    near, far = [], []
    for gz in range(2):
        targets = layer_targets(gz)
        near_z, far_z = HALF * (1 - gz) + np.arange(HALF), HALF * gz + np.arange(HALF)
        near.append(np.kron(banded(WIDE, R2, near_z, targets).T, ay))
        far.append(np.kron(banded(WIDE, R2, far_z, targets[:QZ]).T, ay))
    mx = np.zeros((DX, 128), np.float32)
    mx[:, :QX] = banded(WIDE, R2, x_all, x_coarse)
    mx[:R] = 0
    mx[DX - R :] = 0
    cols = np.arange(MARGIN)
    pad_in, pad_out = ((0, SLOT - MARGIN), (0, SLOT - MARGIN)), ((0, 0), (0, 0))
    wp = []
    for side_in, x_out, outside in (
        ((cols - MARGIN, cols), cols - R2, lambda x: x < 0),
        ((cols + DX - MARGIN, cols + DX), cols + DX - R, lambda x: x >= DX),
    ):
        for masked in (False, True):
            blocks = []
            for x_in in side_in:
                row = []
                for t in (SMOOTH, SLOPE):
                    w = banded(t, R, x_in, x_out)
                    if masked:
                        w = np.where(outside(x_out)[None, :], np.float32(0.0), w)
                    row.append(np.kron(np.eye(8, dtype=np.float32), np.pad(w, pad_in)))
                blocks.append(np.concatenate(row, axis=1))
            wp.append(np.concatenate(blocks, axis=0))
    wz, wzx = [], []
    one = np.eye(SLOT, dtype=np.float32)
    for gz in range(2):
        z_halo = DZ + np.arange(8) if gz == 0 else np.arange(8) - R
        rows = []
        for z_in, used in ((np.arange(DZ), DZ), (z_halo, R)):
            keep = (np.arange(len(z_in)) < used)[:, None]
            rows.append(
                np.concatenate(
                    [np.kron(banded(t, R, z_in, np.arange(DZ)) * keep, one) for t in (SMOOTH, SLOPE)], axis=1
                )
            )
        wz.append(np.concatenate(rows, axis=0))
        bz = banded(WIDE, R2, np.arange(DZ), layer_targets(gz))
        sides = []
        for x_out in (cols - R2, cols + DX - R):
            bx = np.zeros((SLOT, 128), np.float32)
            bx[:MARGIN, :QX] = banded(WIDE, R2, x_out, x_coarse)
            sides.append(np.kron(bz, bx))
        wzx.append(np.concatenate(sides, axis=0))
    named = {"ty": ty, "xp": [x_pair.reshape(2 * DX, DX)], "near": near, "far": far, "mx": [mx], "wp": wp, "wz": wz, "ay": [ay], "wzx": wzx}
    return pack_table(named)


def pack_table(named):
    blocks, places, at = [], {}, 0
    for name, variants in named.items():
        rows, lanes = variants[0].shape
        cuts = -(-lanes // 256)
        places[name] = (at, rows, cuts)
        for m in variants:
            wide = np.pad(np.asarray(m, np.float32), ((0, 0), (0, 256 * cuts - lanes)))
            blocks += [wide[:, 256 * i : 256 * i + 256] for i in range(cuts)]
            at += rows * cuts
    return np.concatenate(blocks, axis=0).astype(BF16), places


def mm(a, b):
    return jnp.dot(a, b, preferred_element_type=F32)


def kernel(
    n_row, n_col, places,
    vol, table,
    out,
    f, strips, strips_z, send_z, zs, zd, planes, grads, prods, acc, panel, xpanel, zpanel, gpanel, psend, precv,
    ty, xp, near, far, mx, wpl, wpr, wz, ay, wzx,
    local_sem, send_sem, recv_sem,
):
    gz, row, col = lax.axis_index("gz"), lax.axis_index("row"), lax.axis_index("col")
    has = {(1, -1): row > 0, (1, 1): row < n_row - 1, (2, -1): col > 0, (2, 1): col < n_col - 1}

    def exists(o):
        tests = [has[d, o[d]] for d in (1, 2) if o[d]]
        if not tests:
            return None
        return tests[0] if len(tests) == 1 else tests[0] & tests[1]

    def when(o, fn):
        ok = exists(o)
        if ok is None:
            fn()
        else:
            pl.when(ok)(fn)

    def peer(o):
        return (lax.rem(gz + o[0], 2), row + o[1], col + o[2])

    barrier = pltpu.get_barrier_semaphore()
    count = 0
    for o in NEIGHBOURS:
        when(o, lambda o=o: pl.semaphore_signal(barrier, inc=1, device_id=peer(o), device_id_type=MESH))
        ok = exists(o)
        count = count + (1 if ok is None else ok.astype(jnp.int32))

    own_z, own_y = pl.ds(R, DZ), pl.ds(16, DY)
    first_y, last_y, top_y, bottom_y = pl.ds(16, 16), pl.ds(DY, 16), pl.ds(0, 16), pl.ds(DY + 16, 16)
    load = pltpu.make_async_copy(vol, f.at[own_z, own_y], local_sem.at[0])
    load.start()
    edge = jnp.where(row == 0, 0, jnp.where(row == n_row - 1, 2, 1))
    fetches = []
    for name, variant, target in (
        ("ty", edge, ty), ("xp", 0, xp), ("near", gz, near), ("far", gz, far), ("mx", 0, mx),
        ("wp", (col == 0).astype(jnp.int32), wpl), ("wp", 2 + (col == n_col - 1).astype(jnp.int32), wpr),
        ("wz", gz, wz), ("ay", 0, ay), ("wzx", gz, wzx),
    ):
        base, rows, cuts = places[name]
        for i in range(cuts):
            start = pl.multiple_of(base + rows * (cuts * variant + i), 16)
            fetches.append(
                pltpu.make_async_copy(
                    table.at[pl.ds(start, rows)], target.at[:, pl.ds(256 * i, 256)], local_sem.at[1 + len(fetches)]
                )
            )
    for c in fetches:
        c.start()

    dead_z = pl.ds((R + DZ) * gz, R)
    f[dead_z] = jnp.zeros((R, WY, DX), jnp.bfloat16)
    for d, where_y in ((-1, top_y), (1, bottom_y)):
        @pl.when(jnp.logical_not(has[1, d]))
        def _(where_y=where_y):
            f[:, where_y] = jnp.zeros((DZ + 2 * R, 16, DX), jnp.bfloat16)
            strips[:, where_y] = jnp.zeros((4, 16, 256), jnp.bfloat16)
            strips_z[:, where_y] = jnp.zeros((4, 16, 128), jnp.bfloat16)
    for d, kind in ((-1, 0), (1, 3)):
        @pl.when(jnp.logical_not(has[2, d]))
        def _(kind=kind):
            strips[kind] = jnp.zeros((WY, 256), jnp.bfloat16)
            strips_z[kind] = jnp.zeros((WY, 128), jnp.bfloat16)

    load.wait()
    near_z = 13 * (1 - gz)

    def pack(layers):
        lane = lax.broadcasted_iota(jnp.int32, (DY, 128), 1)
        first, last = (jnp.zeros((DY, 128), F32) for _ in range(2))
        for t, z in enumerate(layers):
            tile = f[R + z, 16 : 16 + DY, :]
            use = (lane >= SLOT * t) & (lane < SLOT * t + MARGIN)
            first = jnp.where(use, pltpu.roll(tile[:, :128].astype(F32), SLOT * t, 1), first)
            last = jnp.where(use, pltpu.roll(tile[:, 128:].astype(F32), (SLOT * t + MARGIN) % 128, 1), last)
        return first.astype(jnp.bfloat16), last.astype(jnp.bfloat16)

    for h in range(2):
        first, last = pack([HALF * h + t for t in range(8)])
        strips[1, 16 : 16 + DY, 128 * h : 128 * h + 128] = first
        strips[2, 16 : 16 + DY, 128 * h : 128 * h + 128] = last
    first, last = pack([near_z + t for t in range(R)])
    send_z[0] = first
    send_z[1] = last

    messages = []

    def message(o, source, target):
        i = len(messages)
        c = pltpu.make_async_remote_copy(
            src_ref=source, dst_ref=target, send_sem=send_sem.at[i], recv_sem=recv_sem.at[i],
            device_id=peer(o), device_id_type=MESH,
        )
        messages.append((o, c))

    near_layers, halo_layers = pl.ds(near_z, R), pl.ds((R + DZ) * gz, R)
    both = pl.ds(0, 2)
    own_kinds = pl.ds(1, 2)
    y_cut = {0: (pl.ds(0, DY), own_y), 1: (pl.ds(DY - 16, 16), top_y), -1: (pl.ds(0, 16), bottom_y)}
    for o in sorted(NEIGHBOURS, key=lambda o: -(2 * o[0] + abs(o[1]) + abs(o[2])) - 9 * (o == (1, 0, 0))):
        a, b, c = o
        src_y, dst_y = y_cut[b]
        strip_y = pl.ds(16 + (DY - 16 if b == 1 else 0), DY if b == 0 else 16)
        if c == 0 and a == 0:
            message(o, vol.at[:, src_y], f.at[own_z, dst_y])
            message(o, strips.at[own_kinds, strip_y], strips.at[own_kinds, dst_y])
        elif c == 0:
            message(o, vol.at[near_layers, src_y], f.at[halo_layers, dst_y])
            message(o, send_z.at[both, src_y], strips_z.at[own_kinds, dst_y])
        else:
            mine, theirs = (2, 0) if c == 1 else (1, 3)
            if a == 0:
                message(o, strips.at[mine, strip_y], strips.at[theirs, dst_y])
            else:
                message(o, send_z.at[mine - 1, src_y], strips_z.at[theirs, dst_y])

    pl.semaphore_wait(barrier, count)
    for o, c in messages:
        when(o, lambda c=c: c.start())
    for c in fetches:
        c.wait()
    for o, c in messages:
        when((o[0], -o[1], -o[2]), lambda c=c: c.wait_recv())

    def products(get, put):
        g = [get(i) for i in range(3)]
        for c, (i, j) in enumerate(pair_table):
            put(c, g[i] * g[j])

    for side, (k, w) in enumerate(((0, wpl), (2, wpr))):
        for t in range(3):
            src = [(strips[i, :, 128 * t : 128 * t + 128] if t < 2 else strips_z[i]) for i in (k, k + 1)]
            xs = mm(jnp.concatenate(src, axis=1), w[...]).astype(jnp.bfloat16)
            xpanel[0, :, 128 * t : 128 * t + 128] = xs[:, :128]
            xpanel[1, :, 128 * t : 128 * t + 128] = xs[:, 128:]
        zpanel[0] = mm(xpanel[1], wz[:, :256]).astype(jnp.bfloat16)
        zpanel[1] = mm(xpanel[0], wz[:, :256]).astype(jnp.bfloat16)
        zpanel[2] = mm(xpanel[0], wz[:, 256:]).astype(jnp.bfloat16)
        edge_grads = [
            mm(ty[:GY, :WY] if i != 1 else ty[GY:, :WY], zpanel[i]).astype(jnp.bfloat16) for i in range(3)
        ]

        def put(c, p, side=side):
            gpanel[16 * c : 16 * c + 16, 256 * side : 256 * side + 256] = mm(ay[:, :GY], p).astype(jnp.bfloat16)

        products(lambda i: edge_grads[i], put)
    panel[...] = mm(gpanel[...], wzx[...])

    def gradients(z_base):
        def four_layers(g, _):
            z0 = z_base + 4 * g
            for y in range(0, WY, 16):
                for x in range(0, DX, 128):
                    v = [f[z0 + i, y : y + 16, x : x + 128].astype(F32) for i in range(4 + 2 * R)]
                    for j in range(4):
                        c = v[j : j + 7]
                        smooth, slope = c[3] * float(SMOOTH[R]), None
                        for s in (1, 2, 3):
                            smooth = smooth + (c[3 - s] + c[3 + s]) * float(SMOOTH[R + s])
                            term = (c[3 + s] - c[3 - s]) * float(SLOPE[R + s])
                            slope = term if slope is None else slope + term
                        zs[j, y : y + 16, x : x + 128] = smooth.astype(jnp.bfloat16)
                        zd[j, y : y + 16, x : x + 128] = slope.astype(jnp.bfloat16)
            for j in range(4):
                pair = mm(ty[:, :WY], zs[j]).astype(jnp.bfloat16)
                at = slice(GY * j, GY * j + GY)
                planes[0, at] = pair[:GY]
                planes[1, at] = pair[GY:]
                planes[2, at] = mm(ty[:GY, :WY], zd[j]).astype(jnp.bfloat16)
            for i in range(3):
                grads[i] = mm(planes[i], xp[:DX] if i == 0 else xp[DX:]).astype(jnp.bfloat16)
            for y in range(0, 4 * GY, 16):
                at = pl.ds(pl.multiple_of(4 * GY * g, 16) + y, 16)

                def put(c, p, at=at):
                    prods[c, at] = p

                products(lambda i, y=y: grads[i, y : y + 16], put)
            return 0

        lax.fori_loop(0, 2, four_layers, 0)

    gradients(HALF * (1 - gz))
    for c in range(6):
        s = mm(near[:, : HALF * GY], prods[c])
        acc[c] = s[: QZ * QY]
        reach = mm(s[QZ * QY :].astype(jnp.bfloat16), mx[:, :128])
        for q in range(2):
            edge_part = panel[16 * c : 16 * c + 16, 128 * (QZ + q) : 128 * (QZ + q) + 128]
            psend[c, 16 * q : 16 * q + 16] = (reach[16 * q : 16 * q + 16] + edge_part).astype(jnp.bfloat16)
    message((1, 0, 0), psend, precv)
    messages[-1][1].start()

    gradients(HALF * gz)
    for c in range(6):
        s = acc[c] + mm(far[:, : HALF * GY], prods[c])
        own = mm(s.astype(jnp.bfloat16), mx[:, :128])
        for q in range(QZ):
            part = own[16 * q : 16 * q + 16] + panel[16 * c : 16 * c + 16, 128 * q : 128 * q + 128]
            out[c, q] = part[:, :QX]
    messages[-1][1].wait_recv()
    for q in range(2):
        for c in range(6):
            got = precv[c, 16 * q : 16 * q + 16, :QX].astype(F32)
            out[c, 2 * (1 - gz) + q] += got
    for o, c in messages:
        when(o, lambda c=c: c.wait_send())


def solution(mesh):
    n_row, n_col = mesh.shape["row"], mesh.shape["col"]
    table, places = constants()
    bf = jnp.bfloat16
    hbm = pl.BlockSpec(memory_space=pltpu.HBM)

    def per_device(volume):
        return pl.pallas_call(
            lambda *refs: kernel(n_row, n_col, places, *refs),
            name="structure_tensor",
            out_shape=jax.ShapeDtypeStruct((6, QZ, QY, QX), F32),
            in_specs=[hbm, hbm],
            out_specs=pl.BlockSpec(memory_space=pltpu.VMEM),
            scratch_shapes=[
                pltpu.VMEM((DZ + 2 * R, WY, DX), bf),
                pltpu.VMEM((4, WY, 256), bf),
                pltpu.VMEM((4, WY, 128), bf),
                pltpu.VMEM((2, DY, 128), bf),
                pltpu.VMEM((4, WY, DX), bf),
                pltpu.VMEM((4, WY, DX), bf),
                pltpu.VMEM((3, 4 * GY, DX), bf),
                pltpu.VMEM((3, 4 * GY, DX), bf),
                pltpu.VMEM((6, HALF * GY, DX), bf),
                pltpu.VMEM((6, QZ * QY, DX), F32),
                pltpu.VMEM((96, 768), F32),
                pltpu.VMEM((2, WY, 384), bf),
                pltpu.VMEM((3, WY, 256), bf),
                pltpu.VMEM((96, 512), bf),
                pltpu.VMEM((6, 32, 128), bf),
                pltpu.VMEM((6, 32, 128), bf),
                pltpu.VMEM((2 * GY, 256), bf),
                pltpu.VMEM((2 * DX, DX), bf),
                pltpu.VMEM((6 * 16, 768), bf),
                pltpu.VMEM((4 * 16, 768), bf),
                pltpu.VMEM((DX, 256), bf),
                pltpu.VMEM((256, 256), bf),
                pltpu.VMEM((256, 256), bf),
                pltpu.VMEM((384, 512), bf),
                pltpu.VMEM((16, 256), bf),
                pltpu.VMEM((512, 768), bf),
                pltpu.SemaphoreType.DMA((20,)),
                pltpu.SemaphoreType.DMA((23,)),
                pltpu.SemaphoreType.DMA((23,)),
            ],
            compiler_params=pltpu.CompilerParams(
                collective_id=0, has_side_effects=True, vmem_limit_bytes=VMEM_BYTES
            ),
        )(*[pltpu.with_memory_space_constraint(a, pltpu.HBM) for a in (volume, jnp.asarray(table))])

    return jax.shard_map(
        per_device,
        mesh=mesh,
        in_specs=(P("gz", "row", "col"),),
        out_specs=P(None, "gz", "row", "col"),
        check_vma=False,
    )
```

```python
import itertools

import jax
import jax.numpy as jnp
import ml_dtypes
import numpy as np
from jax import lax
from jax.experimental import pallas as pl
from jax.experimental.pallas import tpu as pltpu
from jax.sharding import PartitionSpec as P

R = 3
R2 = 8
MARGIN = R + R2
BF16 = ml_dtypes.bfloat16
F32 = jnp.float32
MESH = pl.DeviceIdType.MESH

DZ, DY, DX = 16, 64, 256
WY, GY = DY + 32, DY + 2 * R2
QZ, QY, QX = DZ // 4, DY // 4, DX // 4
SLOT = 16
HALF = DZ // 2
GROUP = 4
VMEM_BYTES = 32 * 2**20
NEIGHBOURS = tuple(o for o in itertools.product((0, 1), (-1, 0, 1), (-1, 0, 1)) if o != (0, 0, 0))
pair_table = ((0, 0), (1, 1), (2, 2), (0, 1), (0, 2), (1, 2))


def gauss_taps(radius):
    offsets = np.arange(-radius, radius + 1).astype(np.float32)
    spread = np.float32(radius / 3.0)
    smooth = np.exp(-offsets * offsets / (np.float32(2.0) * spread * spread))
    smooth = smooth / np.sum(smooth)
    slopes = offsets * smooth
    slopes = slopes / np.sum(offsets * slopes)
    return [t.astype(BF16).astype(np.float32) for t in (smooth, slopes)]


SMOOTH, SLOPE = gauss_taps(R)
WIDE, _ = gauss_taps(R2)


def banded(taps, radius, source, target):
    s = np.asarray(source)[:, None] - np.asarray(target)[None, :]
    picked = taps[np.clip(s + radius, 0, 2 * radius)]
    return np.where(np.abs(s) <= radius, picked, np.float32(0.0))


def layer_targets(gz):
    return [0, 4, 8, 12] + ([16, 20] if gz == 0 else [-8, -4])


def near_groups(gz):
    return HALF - GROUP * gz, (DZ - GROUP) * (1 - gz)


def constants():
    y_in, y_out, y_coarse = np.arange(WY) - 16, np.arange(GY) - R2, 4 * np.arange(QY)
    x_all, x_coarse = np.arange(DX), 4 * np.arange(QX)
    ty = []
    for edge in range(3):
        inside = np.ones(GY, np.float32)
        if edge == 0:
            inside[y_out < 0] = 0
        if edge == 2:
            inside[y_out >= DY] = 0
        ty.append(np.concatenate([banded(t, R, y_in, y_out).T * inside[:, None] for t in (SMOOTH, SLOPE)]))
    x_pair = np.stack([banded(SLOPE, R, x_all, x_all), banded(SMOOTH, R, x_all, x_all)])
    ay = banded(WIDE, R2, y_out, y_coarse).T
    near, far = [], []
    for gz in range(2):
        targets = layer_targets(gz)
        far_z = HALF * gz + np.arange(HALF)
        for z0 in near_groups(gz):
            near.append(np.kron(banded(WIDE, R2, z0 + np.arange(GROUP), targets).T, ay))
        far.append(np.kron(banded(WIDE, R2, far_z, targets[:QZ]).T, ay))
    mx = np.zeros((DX, 128), np.float32)
    mx[:, :QX] = banded(WIDE, R2, x_all, x_coarse)
    mx[:R] = 0
    mx[DX - R :] = 0
    cols = np.arange(MARGIN)
    pad_in, pad_out = ((0, SLOT - MARGIN), (0, SLOT - MARGIN)), ((0, 0), (0, 0))
    wp = []
    for side_in, x_out, outside in (
        ((cols - MARGIN, cols), cols - R2, lambda x: x < 0),
        ((cols + DX - MARGIN, cols + DX), cols + DX - R, lambda x: x >= DX),
    ):
        for masked in (False, True):
            blocks = []
            for x_in in side_in:
                row = []
                for t in (SMOOTH, SLOPE):
                    w = banded(t, R, x_in, x_out)
                    if masked:
                        w = np.where(outside(x_out)[None, :], np.float32(0.0), w)
                    row.append(np.kron(np.eye(8, dtype=np.float32), np.pad(w, pad_in)))
                blocks.append(np.concatenate(row, axis=1))
            wp.append(np.concatenate(blocks, axis=0))
    wz, wzx = [], []
    one = np.eye(SLOT, dtype=np.float32)
    for gz in range(2):
        z_halo = DZ + np.arange(8) if gz == 0 else np.arange(8) - R
        rows = []
        for z_in, used in ((np.arange(DZ), DZ), (z_halo, R)):
            keep = (np.arange(len(z_in)) < used)[:, None]
            rows.append(
                np.concatenate(
                    [np.kron(banded(t, R, z_in, np.arange(DZ)) * keep, one) for t in (SMOOTH, SLOPE)], axis=1
                )
            )
        wz.append(np.concatenate(rows, axis=0))
        bz = banded(WIDE, R2, np.arange(DZ), layer_targets(gz))
        sides = []
        for x_out in (cols - R2, cols + DX - R):
            bx = np.zeros((SLOT, 128), np.float32)
            bx[:MARGIN, :QX] = banded(WIDE, R2, x_out, x_coarse)
            sides.append(np.kron(bz, bx))
        wzx.append(np.concatenate(sides, axis=0))
    named = {"ty": ty, "xp": [x_pair.reshape(2 * DX, DX)], "near": near, "far": far, "mx": [mx], "wp": wp, "wz": wz, "ay": [ay], "wzx": wzx}
    return pack_table(named)


def pack_table(named):
    blocks, places, at = [], {}, 0
    for name, variants in named.items():
        rows, lanes = variants[0].shape
        cuts = -(-lanes // 256)
        places[name] = (at, rows, cuts)
        for m in variants:
            wide = np.pad(np.asarray(m, np.float32), ((0, 0), (0, 256 * cuts - lanes)))
            blocks += [wide[:, 256 * i : 256 * i + 256] for i in range(cuts)]
            at += rows * cuts
    return np.concatenate(blocks, axis=0).astype(BF16), places


def mm(a, b):
    return jnp.dot(a, b, preferred_element_type=F32)


def kernel(
    n_row, n_col, places,
    vol, table,
    out,
    f, strips, strips_z, send_z, zs_all, zd_all, planes_all, grads_all, prods, acc, xpanel, zpanel, gpanel, psend, precv,
    ty, xp, near_a, near_b, far, mx, wpl, wpr, wz, ay, wzx,
    local_sem, send_sem, recv_sem,
):
    gz, row, col = lax.axis_index("gz"), lax.axis_index("row"), lax.axis_index("col")
    has = {(1, -1): row > 0, (1, 1): row < n_row - 1, (2, -1): col > 0, (2, 1): col < n_col - 1}

    def exists(o):
        tests = [has[d, o[d]] for d in (1, 2) if o[d]]
        if not tests:
            return None
        return tests[0] if len(tests) == 1 else tests[0] & tests[1]

    def when(o, fn):
        ok = exists(o)
        if ok is None:
            fn()
        else:
            pl.when(ok)(fn)

    def peer(o):
        return (lax.rem(gz + o[0], 2), row + o[1], col + o[2])

    barrier = pltpu.get_barrier_semaphore()
    count = 0
    for o in NEIGHBOURS:
        when(o, lambda o=o: pl.semaphore_signal(barrier, inc=1, device_id=peer(o), device_id_type=MESH))
        ok = exists(o)
        count = count + (1 if ok is None else ok.astype(jnp.int32))

    own_z, own_y = pl.ds(R, DZ), pl.ds(16, DY)
    first_y, last_y, top_y, bottom_y = pl.ds(16, 16), pl.ds(DY, 16), pl.ds(0, 16), pl.ds(DY + 16, 16)
    load = pltpu.make_async_copy(vol, f.at[own_z, own_y], local_sem.at[0])
    load.start()
    edge = jnp.where(row == 0, 0, jnp.where(row == n_row - 1, 2, 1))
    fetches = []
    for name, variant, target in (
        ("ty", edge, ty), ("xp", 0, xp), ("near", 2 * gz, near_a), ("near", 2 * gz + 1, near_b), ("far", gz, far), ("mx", 0, mx),
        ("wp", (col == 0).astype(jnp.int32), wpl), ("wp", 2 + (col == n_col - 1).astype(jnp.int32), wpr),
        ("wz", gz, wz), ("ay", 0, ay), ("wzx", gz, wzx),
    ):
        base, rows, cuts = places[name]
        for i in range(cuts):
            start = pl.multiple_of(base + rows * (cuts * variant + i), 16)
            fetches.append(
                pltpu.make_async_copy(
                    table.at[pl.ds(start, rows)], target.at[:, pl.ds(256 * i, 256)], local_sem.at[1 + len(fetches)]
                )
            )

    near_z = 13 * (1 - gz)
    messages, raw, packed = [], [], []

    def message(o, source, target, group):
        i = len(messages)
        c = pltpu.make_async_remote_copy(
            src_ref=source, dst_ref=target, send_sem=send_sem.at[i], recv_sem=recv_sem.at[i],
            device_id=peer(o), device_id_type=MESH,
        )
        messages.append((o, c))
        group.append((o, c))

    near_layers, halo_layers = pl.ds(near_z, R), pl.ds((R + DZ) * gz, R)
    both = pl.ds(0, 2)
    own_kinds = pl.ds(1, 2)
    y_cut = {0: (pl.ds(0, DY), own_y), 1: (pl.ds(DY - 16, 16), top_y), -1: (pl.ds(0, 16), bottom_y)}
    for o in sorted(NEIGHBOURS, key=lambda o: -(2 * o[0] + abs(o[1]) + abs(o[2])) - 9 * (o == (1, 0, 0))):
        a, b, c = o
        src_y, dst_y = y_cut[b]
        strip_y = pl.ds(16 + (DY - 16 if b == 1 else 0), DY if b == 0 else 16)
        if c == 0 and a == 0:
            message(o, vol.at[:, src_y], f.at[own_z, dst_y], raw)
            message(o, strips.at[own_kinds, strip_y], strips.at[own_kinds, dst_y], packed)
        elif c == 0:
            message(o, vol.at[near_layers, src_y], f.at[halo_layers, dst_y], raw)
            message(o, send_z.at[both, src_y], strips_z.at[own_kinds, dst_y], packed)
        else:
            mine, theirs = (2, 0) if c == 1 else (1, 3)
            if a == 0:
                message(o, strips.at[mine, strip_y], strips.at[theirs, dst_y], packed)
            else:
                message(o, send_z.at[mine - 1, src_y], strips_z.at[theirs, dst_y], packed)

    for c in fetches:
        c.start()
    dead_z = pl.ds((R + DZ) * gz, R)
    f[dead_z] = jnp.zeros((R, WY, DX), jnp.bfloat16)
    for d, where_y in ((-1, top_y), (1, bottom_y)):
        @pl.when(jnp.logical_not(has[1, d]))
        def _(where_y=where_y):
            f[:, where_y] = jnp.zeros((DZ + 2 * R, 16, DX), jnp.bfloat16)
            strips[:, where_y] = jnp.zeros((4, 16, 256), jnp.bfloat16)
            strips_z[:, where_y] = jnp.zeros((4, 16, 128), jnp.bfloat16)
    for d, kind in ((-1, 0), (1, 3)):
        @pl.when(jnp.logical_not(has[2, d]))
        def _(kind=kind):
            strips[kind] = jnp.zeros((WY, 256), jnp.bfloat16)
            strips_z[kind] = jnp.zeros((WY, 128), jnp.bfloat16)

    load.wait()

    def pack(layers):
        lane = lax.broadcasted_iota(jnp.int32, (DY, 128), 1)
        first, last = (jnp.zeros((DY, 128), F32) for _ in range(2))
        for t, z in enumerate(layers):
            tile = f[R + z, 16 : 16 + DY, :]
            use = (lane >= SLOT * t) & (lane < SLOT * t + MARGIN)
            first = jnp.where(use, pltpu.roll(tile[:, :128].astype(F32), SLOT * t, 1), first)
            last = jnp.where(use, pltpu.roll(tile[:, 128:].astype(F32), (SLOT * t + MARGIN) % 128, 1), last)
        return first.astype(jnp.bfloat16), last.astype(jnp.bfloat16)

    for h in range(2):
        first, last = pack([HALF * h + t for t in range(8)])
        strips[1, 16 : 16 + DY, 128 * h : 128 * h + 128] = first
        strips[2, 16 : 16 + DY, 128 * h : 128 * h + 128] = last
    first, last = pack([near_z + t for t in range(R)])
    send_z[0] = first
    send_z[1] = last

    pl.semaphore_wait(barrier, count)
    for o, c in raw:
        when(o, lambda c=c: c.start())
    for o, c in packed:
        when(o, lambda c=c: c.start())
    for c in fetches:
        c.wait()

    def arrive(group):
        for o, c in group:
            when((o[0], -o[1], -o[2]), lambda c=c: c.wait_recv())

    def products(get, put):
        g = [get(i) for i in range(3)]
        for c, (i, j) in enumerate(pair_table):
            put(c, g[i] * g[j])

    def panel_stages():
        for side, (k, w) in enumerate(((0, wpl), (2, wpr))):
            rows = []
            for t in range(3):
                src = [(strips[i, :, 128 * t : 128 * t + 128] if t < 2 else strips_z[i]) for i in (k, k + 1)]
                rows.append(jnp.concatenate(src, axis=1))
            xs = mm(jnp.concatenate(rows, axis=0), w[...]).astype(jnp.bfloat16)
            for t in range(3):
                part = xs[WY * t : WY * t + WY]
                xpanel[0, WY * side : WY * side + WY, 128 * t : 128 * t + 128] = part[:, :128]
                xpanel[1, WY * side : WY * side + WY, 128 * t : 128 * t + 128] = part[:, 128:]
        yield
        both_z = mm(xpanel[0], wz[...]).astype(jnp.bfloat16)
        zpanel[0] = mm(xpanel[1], wz[:, :256]).astype(jnp.bfloat16)
        zpanel[1] = both_z[:, :256]
        zpanel[2] = both_z[:, 256:]
        yield
        edge_grads = [
            [
                mm(ty[:GY, :WY] if i != 1 else ty[GY:, :WY], zpanel[i, WY * side : WY * side + WY]).astype(jnp.bfloat16)
                for i in range(3)
            ]
            for side in range(2)
        ]
        yield
        for side in range(2):

            def put(c, p, side=side):
                gpanel[16 * c : 16 * c + 16, 256 * side : 256 * side + 256] = mm(ay[:, :GY], p).astype(jnp.bfloat16)

            products(lambda i, side=side: edge_grads[side][i], put)
        yield

    def layer_stages(z0, g):
        zs, zd, planes, grads = zs_all.at[g], zd_all.at[g], planes_all.at[g], grads_all.at[g]
        for y in range(0, WY, 16):
            for x in range(0, DX, 128):
                v = [f[z0 + i, y : y + 16, x : x + 128].astype(F32) for i in range(GROUP + 2 * R)]
                for j in range(GROUP):
                    c = v[j : j + 7]
                    smooth, slope = c[3] * float(SMOOTH[R]), None
                    for s in (1, 2, 3):
                        smooth = smooth + (c[3 - s] + c[3 + s]) * float(SMOOTH[R + s])
                        term = (c[3 + s] - c[3 - s]) * float(SLOPE[R + s])
                        slope = term if slope is None else slope + term
                    zs[j, y : y + 16, x : x + 128] = smooth.astype(jnp.bfloat16)
                    zd[j, y : y + 16, x : x + 128] = slope.astype(jnp.bfloat16)
        yield
        for j in range(GROUP):
            pair = mm(ty[:, :WY], zs[j]).astype(jnp.bfloat16)
            at = slice(GY * j, GY * j + GY)
            planes[0, at] = pair[:GY]
            planes[1, at] = pair[GY:]
            planes[2, at] = mm(ty[:GY, :WY], zd[j]).astype(jnp.bfloat16)
        yield
        for i in range(3):
            grads[i] = mm(planes[i], xp[:DX] if i == 0 else xp[DX:]).astype(jnp.bfloat16)
        yield
        for y in range(0, GROUP * GY, 16):

            def put(c, p, y=y):
                prods[c, GROUP * GY * g + y : GROUP * GY * g + y + 16] = p

            products(lambda i, y=y: grads[i, y : y + 16], put)
        yield

    def interleave(*stages):
        for _ in zip(*stages):
            pass

    part = GROUP * GY
    rows_first = [(o, c) for o, c in raw if o[0] == 0]
    arrive(rows_first)
    interleave(layer_stages(HALF - GROUP * gz, 0))
    for c in range(6):
        acc[c] = mm(near_a[:, :part], prods[c, :part])

    arrive([(o, c) for o, c in raw if o[0] == 1] + packed)
    interleave(panel_stages(), layer_stages((DZ - GROUP) * (1 - gz), 1))
    edge_part = mm(gpanel[...], wzx[:, 128 * QZ :])
    for c in range(6):
        s = acc[c] + mm(near_b[:, :part], prods[c, part:])
        acc[c, : QZ * QY] = s[: QZ * QY]
        reach = mm(s[QZ * QY :].astype(jnp.bfloat16), mx[:, :128])
        for q in range(2):
            edge_q = edge_part[16 * c : 16 * c + 16, 128 * q : 128 * q + 128]
            psend[c, 16 * q : 16 * q + 16] = (reach[16 * q : 16 * q + 16] + edge_q).astype(jnp.bfloat16)
    message((1, 0, 0), psend, precv, [])
    messages[-1][1].start()

    interleave(layer_stages(HALF * gz, 0))
    interleave(layer_stages(HALF * gz + GROUP, 1))
    edge_part = mm(gpanel[...], wzx[:, : 128 * QZ])
    for c in range(6):
        s = acc[c, : QZ * QY] + mm(far[:, : 2 * part], prods[c])
        own = mm(s.astype(jnp.bfloat16), mx[:, :128])
        for q in range(QZ):
            whole = own[16 * q : 16 * q + 16] + edge_part[16 * c : 16 * c + 16, 128 * q : 128 * q + 128]
            out[c, q] = whole[:, :QX]
    messages[-1][1].wait_recv()
    for q in range(2):
        for c in range(6):
            got = precv[c, 16 * q : 16 * q + 16, :QX].astype(F32)
            out[c, 2 * (1 - gz) + q] += got
    for o, c in messages:
        when(o, lambda c=c: c.wait_send())


def solution(mesh):
    n_row, n_col = mesh.shape["row"], mesh.shape["col"]
    table, places = constants()
    bf = jnp.bfloat16
    hbm = pl.BlockSpec(memory_space=pltpu.HBM)

    def per_device(volume):
        return pl.pallas_call(
            lambda *refs: kernel(n_row, n_col, places, *refs),
            name="structure_tensor",
            out_shape=jax.ShapeDtypeStruct((6, QZ, QY, QX), F32),
            in_specs=[hbm, hbm],
            out_specs=pl.BlockSpec(memory_space=pltpu.VMEM),
            scratch_shapes=[
                pltpu.VMEM((DZ + 2 * R, WY, DX), bf),
                pltpu.VMEM((4, WY, 256), bf),
                pltpu.VMEM((4, WY, 128), bf),
                pltpu.VMEM((2, DY, 128), bf),
                pltpu.VMEM((2, 4, WY, DX), bf),
                pltpu.VMEM((2, 4, WY, DX), bf),
                pltpu.VMEM((2, 3, 4 * GY, DX), bf),
                pltpu.VMEM((2, 3, 4 * GY, DX), bf),
                pltpu.VMEM((6, HALF * GY, DX), bf),
                pltpu.VMEM((6, (QZ + 2) * QY, DX), F32),
                pltpu.VMEM((2, 2 * WY, 384), bf),
                pltpu.VMEM((3, 2 * WY, 256), bf),
                pltpu.VMEM((96, 512), bf),
                pltpu.VMEM((6, 32, 128), bf),
                pltpu.VMEM((6, 32, 128), bf),
                pltpu.VMEM((2 * GY, 256), bf),
                pltpu.VMEM((2 * DX, DX), bf),
                pltpu.VMEM((6 * 16, 512), bf),
                pltpu.VMEM((6 * 16, 512), bf),
                pltpu.VMEM((4 * 16, 768), bf),
                pltpu.VMEM((DX, 256), bf),
                pltpu.VMEM((256, 256), bf),
                pltpu.VMEM((256, 256), bf),
                pltpu.VMEM((384, 512), bf),
                pltpu.VMEM((16, 256), bf),
                pltpu.VMEM((512, 768), bf),
                pltpu.SemaphoreType.DMA((20,)),
                pltpu.SemaphoreType.DMA((23,)),
                pltpu.SemaphoreType.DMA((23,)),
            ],
            compiler_params=pltpu.CompilerParams(
                collective_id=0, has_side_effects=True, vmem_limit_bytes=VMEM_BYTES
            ),
        )(*[pltpu.with_memory_space_constraint(a, pltpu.HBM) for a in (volume, jnp.asarray(table))])

    return jax.shard_map(
        per_device,
        mesh=mesh,
        in_specs=(P("gz", "row", "col"),),
        out_specs=P(None, "gz", "row", "col"),
        check_vma=False,
    )
```

```python
import itertools

import jax
import jax.numpy as jnp
import ml_dtypes
import numpy as np
from jax import lax
from jax.experimental import pallas as pl
from jax.experimental.pallas import tpu as pltpu
from jax.sharding import PartitionSpec as P

R = 3
R2 = 8
MARGIN = R + R2
BF16 = ml_dtypes.bfloat16
F32 = jnp.float32
MESH = pl.DeviceIdType.MESH

DZ, DY, DX = 16, 64, 256
WY, GY = DY + 32, DY + 2 * R2
QZ, QY, QX = DZ // 4, DY // 4, DX // 4
SLOT = 16
HALF = DZ // 2
GROUP = 4
VMEM_BYTES = 32 * 2**20
NEIGHBOURS = tuple(o for o in itertools.product((0, 1), (-1, 0, 1), (-1, 0, 1)) if o != (0, 0, 0))
pair_table = ((0, 0), (1, 1), (2, 2), (0, 1), (0, 2), (1, 2))


def gauss_taps(radius):
    offsets = np.arange(-radius, radius + 1).astype(np.float32)
    spread = np.float32(radius / 3.0)
    smooth = np.exp(-offsets * offsets / (np.float32(2.0) * spread * spread))
    smooth = smooth / np.sum(smooth)
    slopes = offsets * smooth
    slopes = slopes / np.sum(offsets * slopes)
    return [t.astype(BF16).astype(np.float32) for t in (smooth, slopes)]


SMOOTH, SLOPE = gauss_taps(R)
WIDE, _ = gauss_taps(R2)


def banded(taps, radius, source, target):
    s = np.asarray(source)[:, None] - np.asarray(target)[None, :]
    picked = taps[np.clip(s + radius, 0, 2 * radius)]
    return np.where(np.abs(s) <= radius, picked, np.float32(0.0))


def layer_targets(gz):
    return [0, 4, 8, 12] + ([16, 20] if gz == 0 else [-8, -4])


def near_groups(gz):
    return HALF - GROUP * gz, (DZ - GROUP) * (1 - gz)


def constants():
    y_in, y_out, y_coarse = np.arange(WY) - 16, np.arange(GY) - R2, 4 * np.arange(QY)
    x_all, x_coarse = np.arange(DX), 4 * np.arange(QX)
    ty = []
    for edge in range(3):
        inside = np.ones(GY, np.float32)
        if edge == 0:
            inside[y_out < 0] = 0
        if edge == 2:
            inside[y_out >= DY] = 0
        ty.append(np.concatenate([banded(t, R, y_in, y_out).T * inside[:, None] for t in (SMOOTH, SLOPE)]))
    x_pair = np.stack([banded(SLOPE, R, x_all, x_all), banded(SMOOTH, R, x_all, x_all)])
    ay = banded(WIDE, R2, y_out, y_coarse).T
    near, far = [], []
    for gz in range(2):
        targets = layer_targets(gz)
        far_z = HALF * gz + np.arange(HALF)
        for z0 in near_groups(gz):
            near.append(np.kron(banded(WIDE, R2, z0 + np.arange(GROUP), targets).T, ay))
        far.append(np.kron(banded(WIDE, R2, far_z, targets[:QZ]).T, ay))
    mx = np.zeros((2, DX, 2, QX), np.float32)
    for i in range(2):
        mx[i, R : DX - R, i] = banded(WIDE, R2, x_all[R : DX - R], x_coarse)
    mx = mx.reshape(2 * DX, 2 * QX)
    cols = np.arange(MARGIN)
    pad_in, pad_out = ((0, SLOT - MARGIN), (0, SLOT - MARGIN)), ((0, 0), (0, 0))
    wp = []
    for side_in, x_out, outside in (
        ((cols - MARGIN, cols), cols - R2, lambda x: x < 0),
        ((cols + DX - MARGIN, cols + DX), cols + DX - R, lambda x: x >= DX),
    ):
        for masked in (False, True):
            blocks = []
            for x_in in side_in:
                row = []
                for t in (SMOOTH, SLOPE):
                    w = banded(t, R, x_in, x_out)
                    if masked:
                        w = np.where(outside(x_out)[None, :], np.float32(0.0), w)
                    row.append(np.kron(np.eye(8, dtype=np.float32), np.pad(w, pad_in)))
                blocks.append(np.concatenate(row, axis=1))
            wp.append(np.concatenate(blocks, axis=0))
    wz, wzx = [], []
    one = np.eye(SLOT, dtype=np.float32)
    for gz in range(2):
        z_halo = DZ + np.arange(8) if gz == 0 else np.arange(8) - R
        rows = []
        for z_in, used in ((np.arange(DZ), DZ), (z_halo, R)):
            keep = (np.arange(len(z_in)) < used)[:, None]
            rows.append(
                np.concatenate(
                    [np.kron(banded(t, R, z_in, np.arange(DZ)) * keep, one) for t in (SMOOTH, SLOPE)], axis=1
                )
            )
        wz.append(np.concatenate(rows, axis=0))
        bz = banded(WIDE, R2, np.arange(DZ), layer_targets(gz))
        sides = []
        for x_out in (cols - R2, cols + DX - R):
            bx = np.zeros((SLOT, 128), np.float32)
            bx[:MARGIN] = np.tile(banded(WIDE, R2, x_out, x_coarse), 2)
            sides.append(np.kron(bz, bx))
        wzx.append(np.concatenate(sides, axis=0))
    named = {"ty": ty, "xp": [x_pair.reshape(2 * DX, DX)], "near": near, "far": far, "mx": [mx], "wp": wp, "wz": wz, "ay": [ay], "wzx": wzx}
    return pack_table(named)


def pack_table(named):
    blocks, places, at = [], {}, 0
    for name, variants in named.items():
        rows, lanes = variants[0].shape
        cuts = -(-lanes // 256)
        places[name] = (at, rows, cuts)
        for m in variants:
            wide = np.pad(np.asarray(m, np.float32), ((0, 0), (0, 256 * cuts - lanes)))
            blocks += [wide[:, 256 * i : 256 * i + 256] for i in range(cuts)]
            at += rows * cuts
    return np.concatenate(blocks, axis=0).astype(BF16), places


def mm(a, b):
    return jnp.dot(a, b, preferred_element_type=F32)


def kernel(
    n_row, n_col, places,
    vol, table,
    out,
    f, strips, strips_z, send_z, fold_send, fold_recv, zs_all, zd_all, planes_all, grads_all, prods, acc, xpanel, zpanel, gpanel, psend, precv,
    ty, xp, near_a, near_b, far, mx, wpl, wpr, wz, ay, wzx,
    local_sem, send_sem, recv_sem,
):
    gz, row, col = lax.axis_index("gz"), lax.axis_index("row"), lax.axis_index("col")
    has = {(1, -1): row > 0, (1, 1): row < n_row - 1, (2, -1): col > 0, (2, 1): col < n_col - 1}

    def exists(o):
        tests = [has[d, o[d]] for d in (1, 2) if o[d]]
        if not tests:
            return None
        return tests[0] if len(tests) == 1 else tests[0] & tests[1]

    def when(o, fn):
        ok = exists(o)
        if ok is None:
            fn()
        else:
            pl.when(ok)(fn)

    def peer(o):
        return (lax.rem(gz + o[0], 2), row + o[1], col + o[2])

    barrier = pltpu.get_barrier_semaphore()
    count = 0
    for o in NEIGHBOURS:
        when(o, lambda o=o: pl.semaphore_signal(barrier, inc=1, device_id=peer(o), device_id_type=MESH))
        ok = exists(o)
        count = count + (1 if ok is None else ok.astype(jnp.int32))

    own_z, own_y = pl.ds(R, DZ), pl.ds(16, DY)
    first_y, last_y, top_y, bottom_y = pl.ds(16, 16), pl.ds(DY, 16), pl.ds(0, 16), pl.ds(DY + 16, 16)
    load = pltpu.make_async_copy(vol, f.at[own_z, own_y], local_sem.at[0])
    load.start()
    edge = jnp.where(row == 0, 0, jnp.where(row == n_row - 1, 2, 1))
    fetches = []
    for name, variant, target in (
        ("ty", edge, ty), ("xp", 0, xp), ("near", 2 * gz, near_a), ("near", 2 * gz + 1, near_b), ("far", gz, far), ("mx", 0, mx),
        ("wp", (col == 0).astype(jnp.int32), wpl), ("wp", 2 + (col == n_col - 1).astype(jnp.int32), wpr),
        ("wz", gz, wz), ("ay", 0, ay), ("wzx", gz, wzx),
    ):
        base, rows, cuts = places[name]
        for i in range(cuts):
            start = pl.multiple_of(base + rows * (cuts * variant + i), 16)
            fetches.append(
                pltpu.make_async_copy(
                    table.at[pl.ds(start, rows)], target.at[:, pl.ds(256 * i, 256)], local_sem.at[1 + len(fetches)]
                )
            )

    near_z = 13 * (1 - gz)
    messages, raw, packed = [], [], []

    def message(o, source, target, group):
        i = len(messages)
        c = pltpu.make_async_remote_copy(
            src_ref=source, dst_ref=target, send_sem=send_sem.at[i], recv_sem=recv_sem.at[i],
            device_id=peer(o), device_id_type=MESH,
        )
        messages.append((o, c))
        group.append((o, c))

    near_layers, halo_layers = pl.ds(near_z, R), pl.ds((R + DZ) * gz, R)
    own_kinds = pl.ds(1, 2)
    y_cut = {0: (pl.ds(0, DY), own_y), 1: (pl.ds(DY - 16, 16), top_y), -1: (pl.ds(0, 16), bottom_y)}
    for o in sorted(NEIGHBOURS, key=lambda o: -(2 * o[0] + abs(o[1]) + abs(o[2])) - 9 * (o == (1, 0, 0))):
        a, b, c = o
        src_y, dst_y = y_cut[b]
        strip_y = pl.ds(16 + (DY - 16 if b == 1 else 0), DY if b == 0 else 16)
        if c == 0 and a == 0:
            message(o, vol.at[:, src_y], f.at[own_z, dst_y], raw)
            message(o, strips.at[own_kinds, strip_y], strips.at[own_kinds, dst_y], packed)
        elif c == 0:
            message(o, vol.at[near_layers, src_y], f.at[halo_layers, dst_y], raw)
        else:
            mine, theirs = (2, 0) if c == 1 else (1, 3)
            if a == 0:
                message(o, strips.at[mine, strip_y], strips.at[theirs, dst_y], packed)
            elif b == 0:
                message(o, fold_send.at[mine - 1], fold_recv.at[theirs // 2], packed)
            else:
                message(o, send_z.at[mine - 1, src_y], strips_z.at[theirs, dst_y], packed)

    for c in fetches:
        c.start()
    dead_z = pl.ds((R + DZ) * gz, R)
    f[dead_z] = jnp.zeros((R, WY, DX), jnp.bfloat16)
    for d, where_y in ((-1, top_y), (1, bottom_y)):
        @pl.when(jnp.logical_not(has[1, d]))
        def _(where_y=where_y):
            f[:, where_y] = jnp.zeros((DZ + 2 * R, 16, DX), jnp.bfloat16)
            strips[:, where_y] = jnp.zeros((4, 16, 256), jnp.bfloat16)
            for kind in (0, 3):
                strips_z[kind, where_y] = jnp.zeros((16, 128), jnp.bfloat16)
    for d, kind in ((-1, 0), (1, 3)):
        @pl.when(jnp.logical_not(has[2, d]))
        def _(kind=kind):
            strips[kind] = jnp.zeros((WY, 256), jnp.bfloat16)
            strips_z[kind] = jnp.zeros((WY, 128), jnp.bfloat16)
            fold_recv[kind // 2] = jnp.zeros((DY // 2, 128), jnp.bfloat16)

    load.wait()

    def pack(layers, y=16, rows=DY):
        lane = lax.broadcasted_iota(jnp.int32, (rows, 128), 1)
        first, last = (jnp.zeros((rows, 128), F32) for _ in range(2))
        for t, z in enumerate(layers):
            tile = f[z, y : y + rows, :]
            use = (lane >= SLOT * t) & (lane < SLOT * t + MARGIN)
            first = jnp.where(use, pltpu.roll(tile[:, :128].astype(F32), SLOT * t, 1), first)
            last = jnp.where(use, pltpu.roll(tile[:, 128:].astype(F32), (SLOT * t + MARGIN) % 128, 1), last)
        return first.astype(jnp.bfloat16), last.astype(jnp.bfloat16)

    for h in range(2):
        first, last = pack([R + HALF * h + t for t in range(8)])
        strips[1, 16 : 16 + DY, 128 * h : 128 * h + 128] = first
        strips[2, 16 : 16 + DY, 128 * h : 128 * h + 128] = last
    for i, packed_z in enumerate(pack([R + near_z + t for t in range(R)])):
        send_z[i] = packed_z
        lower = pltpu.roll(packed_z[DY // 2 :].astype(F32), 64, 1)
        fold_send[i] = (packed_z[: DY // 2].astype(F32) + lower).astype(jnp.bfloat16)

    pl.semaphore_wait(barrier, count)
    for o, c in packed + raw:
        when(o, lambda c=c: c.start())
    for c in fetches:
        c.wait()

    def arrive(group):
        for o, c in group:
            when((o[0], -o[1], -o[2]), lambda c=c: c.wait_recv())

    def products(get, put):
        g = [get(i) for i in range(3)]
        for c, (i, j) in enumerate(pair_table):
            put(c, g[i] * g[j])

    def panel_stages():
        halo_z = (R + DZ) * (1 - gz)
        for i, packed_z in enumerate(pack([halo_z + t for t in range(R)], 0, WY)):
            strips_z[1 + i] = packed_z
            strips_z[3 * i, 16 : 16 + DY // 2] = fold_recv[i]
            strips_z[3 * i, 16 + DY // 2 : 16 + DY] = pltpu.roll(fold_recv[i].astype(F32), 64, 1).astype(jnp.bfloat16)
        for side, (k, w) in enumerate(((0, wpl), (2, wpr))):
            rows = []
            for t in range(3):
                src = [(strips[i, :, 128 * t : 128 * t + 128] if t < 2 else strips_z[i]) for i in (k, k + 1)]
                rows.append(jnp.concatenate(src, axis=1))
            xs = mm(jnp.concatenate(rows, axis=0), w[...]).astype(jnp.bfloat16)
            for t in range(3):
                part = xs[WY * t : WY * t + WY]
                xpanel[0, WY * side : WY * side + WY, 128 * t : 128 * t + 128] = part[:, :128]
                xpanel[1, WY * side : WY * side + WY, 128 * t : 128 * t + 128] = part[:, 128:]
        yield
        both_z = mm(xpanel[0], wz[...]).astype(jnp.bfloat16)
        zpanel[0] = mm(xpanel[1], wz[:, :256]).astype(jnp.bfloat16)
        zpanel[1] = both_z[:, :256]
        zpanel[2] = both_z[:, 256:]
        yield
        edge_grads = [
            [
                mm(ty[:GY, :WY] if i != 1 else ty[GY:, :WY], zpanel[i, WY * side : WY * side + WY]).astype(jnp.bfloat16)
                for i in range(3)
            ]
            for side in range(2)
        ]
        yield
        for side in range(2):

            def put(c, p, side=side):
                gpanel[16 * c : 16 * c + 16, 256 * side : 256 * side + 256] = mm(ay[:, :GY], p).astype(jnp.bfloat16)

            products(lambda i, side=side: edge_grads[side][i], put)
        yield

    def layer_stages(z0, g):
        zs, zd, planes, grads = zs_all.at[g], zd_all.at[g], planes_all.at[g], grads_all.at[g]
        for y in range(0, WY, 16):
            for x in range(0, DX, 128):
                v = [f[z0 + i, y : y + 16, x : x + 128].astype(F32) for i in range(GROUP + 2 * R)]
                for j in range(GROUP):
                    c = v[j : j + 7]
                    smooth, slope = c[3] * float(SMOOTH[R]), None
                    for s in (1, 2, 3):
                        smooth = smooth + (c[3 - s] + c[3 + s]) * float(SMOOTH[R + s])
                        term = (c[3 + s] - c[3 - s]) * float(SLOPE[R + s])
                        slope = term if slope is None else slope + term
                    zs[j, y : y + 16, x : x + 128] = smooth.astype(jnp.bfloat16)
                    zd[j, y : y + 16, x : x + 128] = slope.astype(jnp.bfloat16)
        yield
        for j in range(GROUP):
            pair = mm(ty[:, :WY], zs[j]).astype(jnp.bfloat16)
            at = slice(GY * j, GY * j + GY)
            planes[0, at] = pair[:GY]
            planes[1, at] = pair[GY:]
            planes[2, at] = mm(ty[:GY, :WY], zd[j]).astype(jnp.bfloat16)
        yield
        for i in range(3):
            grads[i] = mm(planes[i], xp[:DX] if i == 0 else xp[DX:]).astype(jnp.bfloat16)
        yield
        for y in range(0, GROUP * GY, 16):

            def put(c, p, y=y):
                prods[c, GROUP * GY * g + y : GROUP * GY * g + y + 16] = p

            products(lambda i, y=y: grads[i, y : y + 16], put)
        yield

    def interleave(*stages):
        for _ in zip(*stages):
            pass

    part = GROUP * GY
    rows_first = [(o, c) for o, c in raw if o[0] == 0]
    arrive(rows_first)
    interleave(layer_stages(HALF - GROUP * gz, 0))
    for c in range(6):
        acc[c] = mm(near_a[:, :part], prods[c, :part])

    arrive([(o, c) for o, c in raw if o[0] == 1] + packed)
    interleave(panel_stages(), layer_stages((DZ - GROUP) * (1 - gz), 1))
    edge_part = mm(gpanel[...], wzx[:, 128 * QZ :])
    low = lax.broadcasted_iota(jnp.int32, (16, 2 * QX), 1) < QX
    for pair in range(3):
        reach = []
        for c in (2 * pair, 2 * pair + 1):
            s = acc[c] + mm(near_b[:, :part], prods[c, part:])
            acc[c, : QZ * QY] = s[: QZ * QY]
            reach.append(s[QZ * QY :].astype(jnp.bfloat16))
        reach = mm(jnp.concatenate(reach, axis=1), mx[:, :128])
        for q in range(2):
            even, odd = (edge_part[16 * c : 16 * c + 16, 128 * q : 128 * q + 128] for c in (2 * pair, 2 * pair + 1))
            psend[pair, 16 * q : 16 * q + 16] = (reach[16 * q : 16 * q + 16] + jnp.where(low, even, odd)).astype(jnp.bfloat16)
    message((1, 0, 0), psend, precv, [])
    messages[-1][1].start()

    interleave(layer_stages(HALF * gz, 0))
    interleave(layer_stages(HALF * gz + GROUP, 1))
    edge_part = mm(gpanel[...], wzx[:, : 128 * QZ])
    for c in range(6):
        s = acc[c, : QZ * QY] + mm(far[:, : 2 * part], prods[c])
        own = mm(s.astype(jnp.bfloat16), mx[:DX, :128])
        for q in range(QZ):
            whole = own[16 * q : 16 * q + 16] + edge_part[16 * c : 16 * c + 16, 128 * q : 128 * q + 128]
            out[c, q] = whole[:, :QX]
    for o, c in messages[:-1]:
        when(o, lambda c=c: c.wait_send())
    messages[-1][1].wait_recv()
    for q in range(2):
        for c in range(6):
            got = precv[c // 2, 16 * q : 16 * q + 16, QX * (c % 2) : QX * (c % 2) + QX].astype(F32)
            out[c, 2 * (1 - gz) + q] += got
    messages[-1][1].wait_send()


def solution(mesh):
    n_row, n_col = mesh.shape["row"], mesh.shape["col"]
    table, places = constants()
    bf = jnp.bfloat16
    hbm = pl.BlockSpec(memory_space=pltpu.HBM)

    def per_device(volume):
        return pl.pallas_call(
            lambda *refs: kernel(n_row, n_col, places, *refs),
            name="structure_tensor",
            out_shape=jax.ShapeDtypeStruct((6, QZ, QY, QX), F32),
            in_specs=[hbm, hbm],
            out_specs=pl.BlockSpec(memory_space=pltpu.VMEM),
            scratch_shapes=[
                pltpu.VMEM((DZ + 2 * R, WY, DX), bf),
                pltpu.VMEM((4, WY, 256), bf),
                pltpu.VMEM((4, WY, 128), bf),
                pltpu.VMEM((2, DY, 128), bf),
                pltpu.VMEM((2, DY // 2, 128), bf),
                pltpu.VMEM((2, DY // 2, 128), bf),
                pltpu.VMEM((2, 4, WY, DX), bf),
                pltpu.VMEM((2, 4, WY, DX), bf),
                pltpu.VMEM((2, 3, 4 * GY, DX), bf),
                pltpu.VMEM((2, 3, 4 * GY, DX), bf),
                pltpu.VMEM((6, HALF * GY, DX), bf),
                pltpu.VMEM((6, (QZ + 2) * QY, DX), F32),
                pltpu.VMEM((2, 2 * WY, 384), bf),
                pltpu.VMEM((3, 2 * WY, 256), bf),
                pltpu.VMEM((96, 512), bf),
                pltpu.VMEM((3, 32, 128), bf),
                pltpu.VMEM((3, 32, 128), bf),
                pltpu.VMEM((2 * GY, 256), bf),
                pltpu.VMEM((2 * DX, DX), bf),
                pltpu.VMEM((6 * 16, 512), bf),
                pltpu.VMEM((6 * 16, 512), bf),
                pltpu.VMEM((4 * 16, 768), bf),
                pltpu.VMEM((2 * DX, 256), bf),
                pltpu.VMEM((256, 256), bf),
                pltpu.VMEM((256, 256), bf),
                pltpu.VMEM((384, 512), bf),
                pltpu.VMEM((16, 256), bf),
                pltpu.VMEM((512, 768), bf),
                pltpu.SemaphoreType.DMA((20,)),
                pltpu.SemaphoreType.DMA((23,)),
                pltpu.SemaphoreType.DMA((23,)),
            ],
            compiler_params=pltpu.CompilerParams(
                collective_id=0, has_side_effects=True, vmem_limit_bytes=VMEM_BYTES
            ),
        )(*[pltpu.with_memory_space_constraint(a, pltpu.HBM) for a in (volume, jnp.asarray(table))])

    return jax.shard_map(
        per_device,
        mesh=mesh,
        in_specs=(P("gz", "row", "col"),),
        out_specs=P(None, "gz", "row", "col"),
        check_vma=False,
    )
```

```python
import itertools

import jax
import jax.numpy as jnp
import ml_dtypes
import numpy as np
from jax import lax
from jax.experimental import pallas as pl
from jax.experimental.pallas import tpu as pltpu
from jax.sharding import PartitionSpec as P

R = 3
R2 = 8
MARGIN = R + R2
BF16 = ml_dtypes.bfloat16
F32 = jnp.float32
MESH = pl.DeviceIdType.MESH

DZ, DY, DX = 16, 64, 256
WY, GY = DY + 32, DY + 2 * R2
QZ, QY, QX = DZ // 4, DY // 4, DX // 4
SLOT = 16
HALF = DZ // 2
GROUPS = (HALF - R, R, HALF // 2, HALF // 2)
STARTS = (0, HALF - R, HALF, HALF + HALF // 2)
DEEPEST = max(GROUPS)
VMEM_BYTES = 32 * 2**20
NEIGHBOURS = tuple(o for o in itertools.product((0, 1), (-1, 0, 1), (-1, 0, 1)) if o != (0, 0, 0))
pair_table = ((0, 0), (1, 1), (2, 2), (0, 1), (0, 2), (1, 2))


def gauss_taps(radius):
    offsets = np.arange(-radius, radius + 1).astype(np.float32)
    spread = np.float32(radius / 3.0)
    smooth = np.exp(-offsets * offsets / (np.float32(2.0) * spread * spread))
    smooth = smooth / np.sum(smooth)
    slopes = offsets * smooth
    slopes = slopes / np.sum(offsets * slopes)
    return [t.astype(BF16).astype(np.float32) for t in (smooth, slopes)]


SMOOTH, SLOPE = gauss_taps(R)
WIDE, _ = gauss_taps(R2)


def banded(taps, radius, source, target):
    s = np.asarray(source)[:, None] - np.asarray(target)[None, :]
    picked = taps[np.clip(s + radius, 0, 2 * radius)]
    return np.where(np.abs(s) <= radius, picked, np.float32(0.0))


def layer_targets(gz):
    return [0, 4, 8, 12] + ([16, 20] if gz == 0 else [-8, -4])


def near_groups(gz):
    return HALF - GROUPS[0] * gz, (DZ - R) * (1 - gz)


def constants():
    y_in, y_out, y_coarse = np.arange(WY) - 16, np.arange(GY) - R2, 4 * np.arange(QY)
    x_all, x_coarse = np.arange(DX), 4 * np.arange(QX)
    ty = []
    for edge in range(3):
        inside = np.ones(GY, np.float32)
        if edge == 0:
            inside[y_out < 0] = 0
        if edge == 2:
            inside[y_out >= DY] = 0
        ty.append(np.concatenate([banded(t, R, y_in, y_out).T * inside[:, None] for t in (SMOOTH, SLOPE)]))
    x_pair = np.stack([banded(SLOPE, R, x_all, x_all), banded(SMOOTH, R, x_all, x_all)])
    ay = banded(WIDE, R2, y_out, y_coarse).T
    near_a, near_b, rest = [], [], []
    for gz in range(2):
        targets = layer_targets(gz)
        a, b = (z0 + np.arange(n) for z0, n in zip(near_groups(gz), GROUPS))
        near_a.append(np.kron(banded(WIDE, R2, a, targets).T, ay))
        near_b.append(np.kron(banded(WIDE, R2, b, targets[QZ:]).T, ay))
        rest_z = np.concatenate([b, HALF * gz + np.arange(HALF)])
        rest.append(np.kron(banded(WIDE, R2, rest_z, targets[:QZ]).T, ay))
    mx = np.zeros((2, DX, 2, QX), np.float32)
    for i in range(2):
        mx[i, R : DX - R, i] = banded(WIDE, R2, x_all[R : DX - R], x_coarse)
    mx = mx.reshape(2 * DX, 2 * QX)
    cols = np.arange(MARGIN)
    pad_in, pad_out = ((0, SLOT - MARGIN), (0, SLOT - MARGIN)), ((0, 0), (0, 0))
    wp = []
    for side_in, x_out, outside in (
        ((cols - MARGIN, cols), cols - R2, lambda x: x < 0),
        ((cols + DX - MARGIN, cols + DX), cols + DX - R, lambda x: x >= DX),
    ):
        for masked in (False, True):
            blocks = []
            for x_in in side_in:
                row = []
                for t in (SMOOTH, SLOPE):
                    w = banded(t, R, x_in, x_out)
                    if masked:
                        w = np.where(outside(x_out)[None, :], np.float32(0.0), w)
                    row.append(np.kron(np.eye(8, dtype=np.float32), np.pad(w, pad_in)))
                blocks.append(np.concatenate(row, axis=1))
            wp.append(np.concatenate(blocks, axis=0))
    wz, wzx = [], []
    one = np.eye(SLOT, dtype=np.float32)
    for gz in range(2):
        z_halo = DZ + np.arange(8) if gz == 0 else np.arange(8) - R
        halves = [HALF * (1 - gz) + np.arange(HALF), HALF * gz + np.arange(HALF)]
        rows = []
        for z_in, used in ((np.arange(DZ), DZ), (z_halo, R)):
            keep = (np.arange(len(z_in)) < used)[:, None]
            rows.append(
                np.concatenate(
                    [np.kron(banded(t, R, z_in, z_out) * keep, one) for z_out in halves for t in (SMOOTH, SLOPE)], axis=1
                )
            )
        wz.append(np.concatenate(rows, axis=0))
        parts = []
        for z_out in halves:
            bz = banded(WIDE, R2, z_out, layer_targets(gz))
            for x_out in (cols - R2, cols + DX - R):
                bx = np.zeros((SLOT, 128), np.float32)
                bx[:MARGIN] = np.tile(banded(WIDE, R2, x_out, x_coarse), 2)
                parts.append(np.kron(bz, bx))
        wzx.append(np.concatenate(parts, axis=0))
    named = {"ty": ty, "xp": [x_pair.reshape(2 * DX, DX)], "near_a": near_a, "near_b": near_b, "rest": rest, "mx": [mx], "wp": wp, "wz": wz, "ay": [ay], "wzx": wzx}
    return pack_table(named)


def pack_table(named):
    blocks, places, at = [], {}, 0
    for name, variants in named.items():
        rows, lanes = variants[0].shape
        cuts = -(-lanes // 256)
        places[name] = (at, rows, cuts)
        for m in variants:
            wide = np.pad(np.asarray(m, np.float32), ((0, 0), (0, 256 * cuts - lanes)))
            blocks += [wide[:, 256 * i : 256 * i + 256] for i in range(cuts)]
            at += rows * cuts
    return np.concatenate(blocks, axis=0).astype(BF16), places


def mm(a, b):
    return jnp.dot(a, b, preferred_element_type=F32)


def kernel(
    n_row, n_col, places,
    vol, table,
    out,
    f, strips, strips_z, send_z, fold_send, fold_recv, zs_all, zd_all, planes_all, grads_all, prods, acc, xpanel, zpanel, gpanel, psend, precv,
    ty, xp, near_a, near_b, rest, mx, wpl, wpr, wz, ay, wzx,
    local_sem, send_sem, recv_sem,
):
    gz, row, col = lax.axis_index("gz"), lax.axis_index("row"), lax.axis_index("col")
    has = {(1, -1): row > 0, (1, 1): row < n_row - 1, (2, -1): col > 0, (2, 1): col < n_col - 1}

    def exists(o):
        tests = [has[d, o[d]] for d in (1, 2) if o[d]]
        if not tests:
            return None
        return tests[0] if len(tests) == 1 else tests[0] & tests[1]

    def when(o, fn):
        ok = exists(o)
        if ok is None:
            fn()
        else:
            pl.when(ok)(fn)

    def peer(o):
        return (lax.rem(gz + o[0], 2), row + o[1], col + o[2])

    barrier = pltpu.get_barrier_semaphore()
    count = 0
    for o in NEIGHBOURS:
        when(o, lambda o=o: pl.semaphore_signal(barrier, inc=1, device_id=peer(o), device_id_type=MESH))
        ok = exists(o)
        count = count + (1 if ok is None else ok.astype(jnp.int32))

    own_z, own_y = pl.ds(R, DZ), pl.ds(16, DY)
    first_y, last_y, top_y, bottom_y = pl.ds(16, 16), pl.ds(DY, 16), pl.ds(0, 16), pl.ds(DY + 16, 16)
    load = pltpu.make_async_copy(vol, f.at[own_z, own_y], local_sem.at[0])
    load.start()
    edge = jnp.where(row == 0, 0, jnp.where(row == n_row - 1, 2, 1))
    fetches = []
    for name, variant, target in (
        ("ty", edge, ty), ("xp", 0, xp), ("near_a", gz, near_a), ("near_b", gz, near_b), ("rest", gz, rest), ("mx", 0, mx),
        ("wp", (col == 0).astype(jnp.int32), wpl), ("wp", 2 + (col == n_col - 1).astype(jnp.int32), wpr),
        ("wz", gz, wz), ("ay", 0, ay), ("wzx", gz, wzx),
    ):
        base, rows, cuts = places[name]
        for i in range(cuts):
            start = pl.multiple_of(base + rows * (cuts * variant + i), 16)
            fetches.append(
                pltpu.make_async_copy(
                    table.at[pl.ds(start, rows)], target.at[:, pl.ds(256 * i, 256)], local_sem.at[1 + len(fetches)]
                )
            )

    near_z = 13 * (1 - gz)
    messages, raw, packed = [], [], []

    def message(o, source, target, group):
        i = len(messages)
        c = pltpu.make_async_remote_copy(
            src_ref=source, dst_ref=target, send_sem=send_sem.at[i], recv_sem=recv_sem.at[i],
            device_id=peer(o), device_id_type=MESH,
        )
        messages.append((o, c))
        group.append((o, c))

    near_layers, halo_layers = pl.ds(near_z, R), pl.ds((R + DZ) * gz, R)
    own_kinds = pl.ds(1, 2)
    y_cut = {0: (pl.ds(0, DY), own_y), 1: (pl.ds(DY - 16, 16), top_y), -1: (pl.ds(0, 16), bottom_y)}
    for o in sorted(NEIGHBOURS, key=lambda o: -(2 * o[0] + abs(o[1]) + abs(o[2])) - 9 * (o == (1, 0, 0))):
        a, b, c = o
        src_y, dst_y = y_cut[b]
        strip_y = pl.ds(16 + (DY - 16 if b == 1 else 0), DY if b == 0 else 16)
        if c == 0 and a == 0:
            message(o, vol.at[:, src_y], f.at[own_z, dst_y], raw)
            message(o, strips.at[own_kinds, strip_y], strips.at[own_kinds, dst_y], packed)
        elif c == 0:
            message(o, vol.at[near_layers, src_y], f.at[halo_layers, dst_y], raw)
        else:
            mine, theirs = (2, 0) if c == 1 else (1, 3)
            if a == 0:
                message(o, strips.at[mine, strip_y], strips.at[theirs, dst_y], packed)
            elif b == 0:
                message(o, fold_send.at[mine - 1], fold_recv.at[theirs // 2], packed)
            else:
                message(o, send_z.at[mine - 1, src_y], strips_z.at[theirs, dst_y], packed)

    for c in fetches:
        c.start()
    dead_z = pl.ds((R + DZ) * gz, R)
    f[dead_z] = jnp.zeros((R, WY, DX), jnp.bfloat16)
    for d, where_y in ((-1, top_y), (1, bottom_y)):
        @pl.when(jnp.logical_not(has[1, d]))
        def _(where_y=where_y):
            f[:, where_y] = jnp.zeros((DZ + 2 * R, 16, DX), jnp.bfloat16)
            strips[:, where_y] = jnp.zeros((4, 16, 256), jnp.bfloat16)
            for kind in (0, 3):
                strips_z[kind, where_y] = jnp.zeros((16, 128), jnp.bfloat16)
    for d, kind in ((-1, 0), (1, 3)):
        @pl.when(jnp.logical_not(has[2, d]))
        def _(kind=kind):
            strips[kind] = jnp.zeros((WY, 256), jnp.bfloat16)
            strips_z[kind] = jnp.zeros((WY, 128), jnp.bfloat16)
            fold_recv[kind // 2] = jnp.zeros((DY // 2, 128), jnp.bfloat16)

    load.wait()

    def pack(layers, y=16, rows=DY):
        lane = lax.broadcasted_iota(jnp.int32, (rows, 128), 1)
        first, last = (jnp.zeros((rows, 128), F32) for _ in range(2))
        for t, z in enumerate(layers):
            tile = f[z, y : y + rows, :]
            use = (lane >= SLOT * t) & (lane < SLOT * t + MARGIN)
            first = jnp.where(use, pltpu.roll(tile[:, :128].astype(F32), SLOT * t, 1), first)
            last = jnp.where(use, pltpu.roll(tile[:, 128:].astype(F32), (SLOT * t + MARGIN) % 128, 1), last)
        return first.astype(jnp.bfloat16), last.astype(jnp.bfloat16)

    for h in range(2):
        first, last = pack([R + HALF * h + t for t in range(8)])
        strips[1, 16 : 16 + DY, 128 * h : 128 * h + 128] = first
        strips[2, 16 : 16 + DY, 128 * h : 128 * h + 128] = last
    for i, packed_z in enumerate(pack([R + near_z + t for t in range(R)])):
        send_z[i] = packed_z
        lower = pltpu.roll(packed_z[DY // 2 :].astype(F32), 64, 1)
        fold_send[i] = (packed_z[: DY // 2].astype(F32) + lower).astype(jnp.bfloat16)

    pl.semaphore_wait(barrier, count)
    for o, c in packed + raw:
        when(o, lambda c=c: c.start())
    for c in fetches:
        c.wait()

    def arrive(group):
        for o, c in group:
            when((o[0], -o[1], -o[2]), lambda c=c: c.wait_recv())

    def products(get, put):
        g = [get(i) for i in range(3)]
        for c, (i, j) in enumerate(pair_table):
            put(c, g[i] * g[j])

    panel_sides = ((0, wpl), (2, wpr))

    def panel_x(tiles):
        for side, (k, w) in enumerate(panel_sides):
            rows = []
            for t in tiles:
                src = [(strips[i, :, 128 * t : 128 * t + 128] if t < 2 else strips_z[i]) for i in (k, k + 1)]
                rows.append(jnp.concatenate(src, axis=1))
            xs = mm(jnp.concatenate(rows, axis=0), w[...]).astype(jnp.bfloat16)
            for i, t in enumerate(tiles):
                piece = xs[WY * i : WY * i + WY]
                xpanel[0, WY * side : WY * side + WY, 128 * t : 128 * t + 128] = piece[:, :128]
                xpanel[1, WY * side : WY * side + WY, 128 * t : 128 * t + 128] = piece[:, 128:]

    def panel_halo():
        halo_z = (R + DZ) * (1 - gz)
        for i, packed_z in enumerate(pack([halo_z + t for t in range(R)], 0, WY)):
            strips_z[1 + i] = packed_z
            strips_z[3 * i, 16 : 16 + DY // 2] = fold_recv[i]
            strips_z[3 * i, 16 + DY // 2 : 16 + DY] = pltpu.roll(fold_recv[i].astype(F32), 64, 1).astype(jnp.bfloat16)
        panel_x((2,))

    def panel_stages(half):
        if half == 0:
            panel_halo()
        yield
        smooth_slope = mm(xpanel[0], wz[:, 256 * half : 256 * half + 256]).astype(jnp.bfloat16)
        zpanel[half, 0] = mm(xpanel[1], wz[:, 256 * half : 256 * half + 128]).astype(jnp.bfloat16)
        zpanel[half, 1] = smooth_slope[:, :128]
        zpanel[half, 2] = smooth_slope[:, 128:]
        yield
        edge_grads = [
            [
                mm(ty[:GY, :WY] if i != 1 else ty[GY:, :WY], zpanel[half, i, WY * side : WY * side + WY]).astype(
                    jnp.bfloat16
                )
                for i in range(3)
            ]
            for side in range(2)
        ]
        yield
        for side in range(2):

            def put(c, p, at=256 * half + 128 * side):
                gpanel[16 * c : 16 * c + 16, at : at + 128] = mm(ay[:, :GY], p).astype(jnp.bfloat16)

            products(lambda i, side=side: edge_grads[side][i], put)
        yield

    def layer_stages(z0, g):
        deep, at_row = GROUPS[g], GY * STARTS[g]
        zs, zd, planes, grads = (ref.at[g % 2] for ref in (zs_all, zd_all, planes_all, grads_all))
        for y in range(0, WY, 16):
            for x in range(0, DX, 128):
                v = [f[z0 + i, y : y + 16, x : x + 128].astype(F32) for i in range(deep + 2 * R)]
                for j in range(deep):
                    c = v[j : j + 7]
                    smooth, slope = c[3] * float(SMOOTH[R]), None
                    for s in (1, 2, 3):
                        smooth = smooth + (c[3 - s] + c[3 + s]) * float(SMOOTH[R + s])
                        term = (c[3 + s] - c[3 - s]) * float(SLOPE[R + s])
                        slope = term if slope is None else slope + term
                    zs[j, y : y + 16, x : x + 128] = smooth.astype(jnp.bfloat16)
                    zd[j, y : y + 16, x : x + 128] = slope.astype(jnp.bfloat16)
        yield
        for j in range(deep):
            pair = mm(ty[:, :WY], zs[j]).astype(jnp.bfloat16)
            at = slice(GY * j, GY * j + GY)
            planes[0, at] = pair[:GY]
            planes[1, at] = pair[GY:]
            planes[2, at] = mm(ty[:GY, :WY], zd[j]).astype(jnp.bfloat16)
        yield
        for i in range(3):
            grads[i, : GY * deep] = mm(planes[i, : GY * deep], xp[:DX] if i == 0 else xp[DX:]).astype(jnp.bfloat16)
        yield
        for y in range(0, GY * deep, 16):

            def put(c, p, y=y):
                prods[c, at_row + y : at_row + y + 16] = p

            products(lambda i, y=y: grads[i, y : y + 16], put)
        yield

    def interleave(*stages):
        for _ in zip(*stages):
            pass

    near_a_z, near_b_z = near_groups(gz)
    ka, kb = GY * GROUPS[0], GY * GROUPS[1]
    rows_first = [(o, c) for o, c in raw if o[0] == 0]
    arrive(rows_first + [(o, c) for o, c in packed if o[0] == 0])
    panel_x((0, 1))
    interleave(layer_stages(near_a_z, 0))
    for c in range(6):
        acc[c] = mm(near_a[:, :ka], prods[c, :ka])

    arrive([m for group in (raw, packed) for m in group if m[0][0] == 1])
    interleave(panel_stages(0), layer_stages(near_b_z, 1))
    edge_part = mm(gpanel[:, :256], wzx[:256, 128 * QZ :])
    low = lax.broadcasted_iota(jnp.int32, (16, 2 * QX), 1) < QX
    for pair in range(3):
        reach = [
            (acc[c, QZ * QY :] + mm(near_b[:, :kb], prods[c, ka : ka + kb])).astype(jnp.bfloat16)
            for c in (2 * pair, 2 * pair + 1)
        ]
        reach = mm(jnp.concatenate(reach, axis=1), mx[:, :128])
        for q in range(2):
            even, odd = (edge_part[16 * c : 16 * c + 16, 128 * q : 128 * q + 128] for c in (2 * pair, 2 * pair + 1))
            psend[pair, 16 * q : 16 * q + 16] = (reach[16 * q : 16 * q + 16] + jnp.where(low, even, odd)).astype(jnp.bfloat16)
    message((1, 0, 0), psend, precv, [])
    messages[-1][1].start()

    interleave(panel_stages(1), layer_stages(HALF * gz, 2))
    interleave(layer_stages(HALF * gz + GROUPS[2], 3))
    edge_part = mm(gpanel[...], wzx[:, : 128 * QZ])
    for c in range(6):
        s = acc[c, : QZ * QY] + mm(rest[:, : DZ * GY - ka], prods[c, ka:])
        own = mm(s.astype(jnp.bfloat16), mx[:DX, :128])
        for q in range(QZ):
            whole = own[16 * q : 16 * q + 16] + edge_part[16 * c : 16 * c + 16, 128 * q : 128 * q + 128]
            out[c, q] = whole[:, :QX]
    for o, c in messages[:-1]:
        when(o, lambda c=c: c.wait_send())
    messages[-1][1].wait_recv()
    for q in range(2):
        for c in range(6):
            got = precv[c // 2, 16 * q : 16 * q + 16, QX * (c % 2) : QX * (c % 2) + QX].astype(F32)
            out[c, 2 * (1 - gz) + q] += got
    messages[-1][1].wait_send()


def solution(mesh):
    n_row, n_col = mesh.shape["row"], mesh.shape["col"]
    table, places = constants()
    bf = jnp.bfloat16
    hbm = pl.BlockSpec(memory_space=pltpu.HBM)

    def per_device(volume):
        return pl.pallas_call(
            lambda *refs: kernel(n_row, n_col, places, *refs),
            name="structure_tensor",
            out_shape=jax.ShapeDtypeStruct((6, QZ, QY, QX), F32),
            in_specs=[hbm, hbm],
            out_specs=pl.BlockSpec(memory_space=pltpu.VMEM),
            scratch_shapes=[
                pltpu.VMEM((DZ + 2 * R, WY, DX), bf),
                pltpu.VMEM((4, WY, 256), bf),
                pltpu.VMEM((4, WY, 128), bf),
                pltpu.VMEM((2, DY, 128), bf),
                pltpu.VMEM((2, DY // 2, 128), bf),
                pltpu.VMEM((2, DY // 2, 128), bf),
                pltpu.VMEM((2, DEEPEST, WY, DX), bf),
                pltpu.VMEM((2, DEEPEST, WY, DX), bf),
                pltpu.VMEM((2, 3, DEEPEST * GY, DX), bf),
                pltpu.VMEM((2, 3, DEEPEST * GY, DX), bf),
                pltpu.VMEM((6, DZ * GY, DX), bf),
                pltpu.VMEM((6, (QZ + 2) * QY, DX), F32),
                pltpu.VMEM((2, 2 * WY, 384), bf),
                pltpu.VMEM((2, 3, 2 * WY, 128), bf),
                pltpu.VMEM((96, 512), bf),
                pltpu.VMEM((3, 32, 128), bf),
                pltpu.VMEM((3, 32, 128), bf),
                pltpu.VMEM((2 * GY, 256), bf),
                pltpu.VMEM((2 * DX, DX), bf),
                pltpu.VMEM((6 * 16, 512), bf),
                pltpu.VMEM((2 * 16, 256), bf),
                pltpu.VMEM((4 * 16, 1024), bf),
                pltpu.VMEM((2 * DX, 256), bf),
                pltpu.VMEM((256, 256), bf),
                pltpu.VMEM((256, 256), bf),
                pltpu.VMEM((384, 512), bf),
                pltpu.VMEM((16, 256), bf),
                pltpu.VMEM((512, 768), bf),
                pltpu.SemaphoreType.DMA((20,)),
                pltpu.SemaphoreType.DMA((23,)),
                pltpu.SemaphoreType.DMA((23,)),
            ],
            compiler_params=pltpu.CompilerParams(
                collective_id=0, has_side_effects=True, vmem_limit_bytes=VMEM_BYTES
            ),
        )(*[pltpu.with_memory_space_constraint(a, pltpu.HBM) for a in (volume, jnp.asarray(table))])

    return jax.shard_map(
        per_device,
        mesh=mesh,
        in_specs=(P("gz", "row", "col"),),
        out_specs=P(None, "gz", "row", "col"),
        check_vma=False,
    )
```

```python
import itertools

import jax
import jax.numpy as jnp
import ml_dtypes
import numpy as np
from jax import lax
from jax.experimental import pallas as pl
from jax.experimental.pallas import tpu as pltpu
from jax.sharding import PartitionSpec as P

R = 3
R2 = 8
MARGIN = R + R2
BF16 = ml_dtypes.bfloat16
F32 = jnp.float32
MESH = pl.DeviceIdType.MESH

DZ, DY, DX = 16, 64, 256
WY, GY = DY + 32, DY + 2 * R2
QZ, QY, QX = DZ // 4, DY // 4, DX // 4
SLOT = 16
HALF = DZ // 2
GROUPS = (HALF - R, R, HALF // 2, HALF // 2)
STARTS = (0, HALF - R, HALF, HALF + HALF // 2)
DEEPEST = max(GROUPS)
VMEM_BYTES = 32 * 2**20
NEIGHBOURS = tuple(o for o in itertools.product((0, 1), (-1, 0, 1), (-1, 0, 1)) if o != (0, 0, 0))
pair_table = ((0, 0), (1, 1), (2, 2), (0, 1), (0, 2), (1, 2))


def gauss_taps(radius):
    offsets = np.arange(-radius, radius + 1).astype(np.float32)
    spread = np.float32(radius / 3.0)
    smooth = np.exp(-offsets * offsets / (np.float32(2.0) * spread * spread))
    smooth = smooth / np.sum(smooth)
    slopes = offsets * smooth
    slopes = slopes / np.sum(offsets * slopes)
    return [t.astype(BF16).astype(np.float32) for t in (smooth, slopes)]


SMOOTH, SLOPE = gauss_taps(R)
WIDE, _ = gauss_taps(R2)


def banded(taps, radius, source, target):
    s = np.asarray(source)[:, None] - np.asarray(target)[None, :]
    picked = taps[np.clip(s + radius, 0, 2 * radius)]
    return np.where(np.abs(s) <= radius, picked, np.float32(0.0))


def layer_targets(gz):
    return [0, 4, 8, 12] + ([16, 20] if gz == 0 else [-8, -4])


def near_groups(gz):
    return HALF - GROUPS[0] * gz, (DZ - R) * (1 - gz)


def constants():
    y_in, y_out, y_coarse = np.arange(WY) - 16, np.arange(GY) - R2, 4 * np.arange(QY)
    x_all, x_coarse = np.arange(DX), 4 * np.arange(QX)
    ty = []
    for edge in range(3):
        inside = np.ones(GY, np.float32)
        if edge == 0:
            inside[y_out < 0] = 0
        if edge == 2:
            inside[y_out >= DY] = 0
        ty.append(np.concatenate([banded(t, R, y_in, y_out).T * inside[:, None] for t in (SMOOTH, SLOPE)]))
    x_pair = np.stack([banded(SLOPE, R, x_all, x_all), banded(SMOOTH, R, x_all, x_all)])
    ay = banded(WIDE, R2, y_out, y_coarse).T
    near_a, near_b, rest = [], [], []
    for gz in range(2):
        targets = layer_targets(gz)
        a, b = (z0 + np.arange(n) for z0, n in zip(near_groups(gz), GROUPS))
        near_a.append(np.kron(banded(WIDE, R2, a, targets).T, ay))
        near_b.append(np.kron(banded(WIDE, R2, b, targets[QZ:]).T, ay))
        rest_z = np.concatenate([b, HALF * gz + np.arange(HALF)])
        rest.append(np.kron(banded(WIDE, R2, rest_z, targets[:QZ]).T, ay))
    mx = np.zeros((2, DX, 2, QX), np.float32)
    for i in range(2):
        mx[i, R : DX - R, i] = banded(WIDE, R2, x_all[R : DX - R], x_coarse)
    mx = mx.reshape(2 * DX, 2 * QX)
    cols = np.arange(MARGIN)
    pad_in, pad_out = ((0, SLOT - MARGIN), (0, SLOT - MARGIN)), ((0, 0), (0, 0))
    wp = []
    for side_in, x_out, outside in (
        ((cols - MARGIN, cols), cols - R2, lambda x: x < 0),
        ((cols + DX - MARGIN, cols + DX), cols + DX - R, lambda x: x >= DX),
    ):
        for masked in (False, True):
            blocks = []
            for x_in in side_in:
                row = []
                for t in (SMOOTH, SLOPE):
                    w = banded(t, R, x_in, x_out)
                    if masked:
                        w = np.where(outside(x_out)[None, :], np.float32(0.0), w)
                    row.append(np.kron(np.eye(8, dtype=np.float32), np.pad(w, pad_in)))
                blocks.append(np.concatenate(row, axis=1))
            wp.append(np.concatenate(blocks, axis=0))
    wz, wzx = [], []
    one = np.eye(SLOT, dtype=np.float32)
    for gz in range(2):
        z_halo = DZ + np.arange(8) if gz == 0 else np.arange(8) - R
        halves = [HALF * (1 - gz) + np.arange(HALF), HALF * gz + np.arange(HALF)]
        rows = []
        for z_in, used in ((np.arange(DZ), DZ), (z_halo, R)):
            keep = (np.arange(len(z_in)) < used)[:, None]
            rows.append(
                np.concatenate(
                    [np.kron(banded(t, R, z_in, z_out) * keep, one) for z_out in halves for t in (SMOOTH, SLOPE)], axis=1
                )
            )
        wz.append(np.concatenate(rows, axis=0))
        parts = []
        for z_out in halves:
            bz = banded(WIDE, R2, z_out, layer_targets(gz))
            for x_out in (cols - R2, cols + DX - R):
                bx = np.zeros((SLOT, 128), np.float32)
                bx[:MARGIN] = np.tile(banded(WIDE, R2, x_out, x_coarse), 2)
                parts.append(np.kron(bz, bx))
        wzx.append(np.concatenate(parts, axis=0))
    named = {"ty": ty, "xp": [x_pair.reshape(2 * DX, DX)], "near_a": near_a, "near_b": near_b, "rest": rest, "mx": [mx], "wp": wp, "wz": wz, "ay": [ay], "wzx": wzx}
    return pack_table(named)


def pack_table(named):
    blocks, places, at = [], {}, 0
    for name, variants in named.items():
        rows, lanes = variants[0].shape
        cuts = -(-lanes // 256)
        places[name] = (at, rows, cuts)
        for m in variants:
            wide = np.pad(np.asarray(m, np.float32), ((0, 0), (0, 256 * cuts - lanes)))
            blocks += [wide[:, 256 * i : 256 * i + 256] for i in range(cuts)]
            at += rows * cuts
    return np.concatenate(blocks, axis=0).astype(BF16), places


def mm(a, b):
    return jnp.dot(a, b, preferred_element_type=F32)


def kernel(
    n_row, n_col, places,
    vol, table,
    out,
    f, strips, strips_z, send_z, fold_send, fold_recv, zs_all, zd_all, planes_all, grads_all, prods, acc, xpanel, zpanel, gpanel, psend, precv,
    ty, xp, near_a, near_b, rest, mx, wpl, wpr, wz, ay, wzx,
    local_sem, send_sem, recv_sem,
):
    gz, row, col = lax.axis_index("gz"), lax.axis_index("row"), lax.axis_index("col")
    has = {(1, -1): row > 0, (1, 1): row < n_row - 1, (2, -1): col > 0, (2, 1): col < n_col - 1}

    def exists(o):
        tests = [has[d, o[d]] for d in (1, 2) if o[d]]
        if not tests:
            return None
        return tests[0] if len(tests) == 1 else tests[0] & tests[1]

    def when(o, fn):
        ok = exists(o)
        if ok is None:
            fn()
        else:
            pl.when(ok)(fn)

    def peer(o):
        return (lax.rem(gz + o[0], 2), row + o[1], col + o[2])

    barrier = pltpu.get_barrier_semaphore()
    count = 0
    for o in NEIGHBOURS:
        when(o, lambda o=o: pl.semaphore_signal(barrier, inc=1, device_id=peer(o), device_id_type=MESH))
        ok = exists(o)
        count = count + (1 if ok is None else ok.astype(jnp.int32))

    own_z, own_y = pl.ds(R, DZ), pl.ds(16, DY)
    first_y, last_y, top_y, bottom_y = pl.ds(16, 16), pl.ds(DY, 16), pl.ds(0, 16), pl.ds(DY + 16, 16)
    load = pltpu.make_async_copy(vol, f.at[own_z, own_y], local_sem.at[0])
    load.start()
    edge = jnp.where(row == 0, 0, jnp.where(row == n_row - 1, 2, 1))
    fetches = []
    for name, variant, target in (
        ("ty", edge, ty), ("xp", 0, xp), ("near_a", gz, near_a), ("near_b", gz, near_b), ("rest", gz, rest), ("mx", 0, mx),
        ("wp", (col == 0).astype(jnp.int32), wpl), ("wp", 2 + (col == n_col - 1).astype(jnp.int32), wpr),
        ("wz", gz, wz), ("ay", 0, ay), ("wzx", gz, wzx),
    ):
        base, rows, cuts = places[name]
        for i in range(cuts):
            start = pl.multiple_of(base + rows * (cuts * variant + i), 16)
            fetches.append(
                pltpu.make_async_copy(
                    table.at[pl.ds(start, rows)], target.at[:, pl.ds(256 * i, 256)], local_sem.at[1 + len(fetches)]
                )
            )

    near_z = 13 * (1 - gz)
    messages, raw, packed = [], [], []

    def message(o, source, target, group):
        i = len(messages)
        c = pltpu.make_async_remote_copy(
            src_ref=source, dst_ref=target, send_sem=send_sem.at[i], recv_sem=recv_sem.at[i],
            device_id=peer(o), device_id_type=MESH,
        )
        messages.append((o, c))
        group.append((o, c))

    near_layers, halo_layers = pl.ds(near_z, R), pl.ds((R + DZ) * gz, R)
    own_kinds = pl.ds(1, 2)
    y_cut = {0: (pl.ds(0, DY), own_y), 1: (pl.ds(DY - 16, 16), top_y), -1: (pl.ds(0, 16), bottom_y)}
    for o in sorted(NEIGHBOURS, key=lambda o: -(2 * o[0] + abs(o[1]) + abs(o[2])) - 9 * (o == (1, 0, 0))):
        a, b, c = o
        src_y, dst_y = y_cut[b]
        strip_y = pl.ds(16 + (DY - 16 if b == 1 else 0), DY if b == 0 else 16)
        if c == 0 and a == 0:
            message(o, vol.at[:, src_y], f.at[own_z, dst_y], raw)
            message(o, strips.at[own_kinds, strip_y], strips.at[own_kinds, dst_y], packed)
        elif c == 0:
            message(o, vol.at[near_layers, src_y], f.at[halo_layers, dst_y], raw)
        else:
            mine, theirs = (2, 0) if c == 1 else (1, 3)
            if a == 0:
                message(o, strips.at[mine, strip_y], strips.at[theirs, dst_y], packed)
            elif b == 0:
                message(o, fold_send.at[mine - 1], fold_recv.at[theirs // 2], packed)
            else:
                message(o, send_z.at[mine - 1, src_y], strips_z.at[theirs, dst_y], packed)

    for c in fetches:
        c.start()
    dead_z = pl.ds((R + DZ) * gz, R)
    f[dead_z] = jnp.zeros((R, WY, DX), jnp.bfloat16)
    for d, where_y in ((-1, top_y), (1, bottom_y)):
        @pl.when(jnp.logical_not(has[1, d]))
        def _(where_y=where_y):
            f[:, where_y] = jnp.zeros((DZ + 2 * R, 16, DX), jnp.bfloat16)
            strips[:, where_y] = jnp.zeros((4, 16, 256), jnp.bfloat16)
            for kind in (0, 3):
                strips_z[kind, where_y] = jnp.zeros((16, 128), jnp.bfloat16)
    for d, kind in ((-1, 0), (1, 3)):
        @pl.when(jnp.logical_not(has[2, d]))
        def _(kind=kind):
            strips[kind] = jnp.zeros((WY, 256), jnp.bfloat16)
            strips_z[kind] = jnp.zeros((WY, 128), jnp.bfloat16)
            fold_recv[kind // 2] = jnp.zeros((DY // 2, 128), jnp.bfloat16)

    load.wait()

    def pack(layers, y=16, rows=DY):
        lane = lax.broadcasted_iota(jnp.int32, (rows, 128), 1)
        first, last = (jnp.zeros((rows, 128), F32) for _ in range(2))
        for t, z in enumerate(layers):
            tile = f[z, y : y + rows, :]
            use = (lane >= SLOT * t) & (lane < SLOT * t + MARGIN)
            first = jnp.where(use, pltpu.roll(tile[:, :128].astype(F32), SLOT * t, 1), first)
            last = jnp.where(use, pltpu.roll(tile[:, 128:].astype(F32), (SLOT * t + MARGIN) % 128, 1), last)
        return first.astype(jnp.bfloat16), last.astype(jnp.bfloat16)

    for h in range(2):
        first, last = pack([R + HALF * h + t for t in range(8)])
        strips[1, 16 : 16 + DY, 128 * h : 128 * h + 128] = first
        strips[2, 16 : 16 + DY, 128 * h : 128 * h + 128] = last
    for i, packed_z in enumerate(pack([R + near_z + t for t in range(R)])):
        send_z[i] = packed_z
        lower = pltpu.roll(packed_z[DY // 2 :].astype(F32), 64, 1)
        fold_send[i] = (packed_z[: DY // 2].astype(F32) + lower).astype(jnp.bfloat16)

    pl.semaphore_wait(barrier, count)
    for o, c in packed + raw:
        when(o, lambda c=c: c.start())
    for c in fetches:
        c.wait()

    def arrive(group):
        for o, c in group:
            when((o[0], -o[1], -o[2]), lambda c=c: c.wait_recv())

    def products(get, put):
        g = [get(i) for i in range(3)]
        for c, (i, j) in enumerate(pair_table):
            put(c, g[i] * g[j])

    panel_sides = ((0, wpl), (2, wpr))

    def panel_x(tiles):
        for side, (k, w) in enumerate(panel_sides):
            rows = []
            for t in tiles:
                src = [(strips[i, :, 128 * t : 128 * t + 128] if t < 2 else strips_z[i]) for i in (k, k + 1)]
                rows.append(jnp.concatenate(src, axis=1))
            xs = mm(jnp.concatenate(rows, axis=0), w[...]).astype(jnp.bfloat16)
            for i, t in enumerate(tiles):
                piece = xs[WY * i : WY * i + WY]
                xpanel[0, WY * side : WY * side + WY, 128 * t : 128 * t + 128] = piece[:, :128]
                xpanel[1, WY * side : WY * side + WY, 128 * t : 128 * t + 128] = piece[:, 128:]

    def pack_halo(y, rows):
        halo_z = (R + DZ) * (1 - gz)
        for i, packed_z in enumerate(pack([halo_z + t for t in range(R)], y, rows)):
            strips_z[1 + i, y : y + rows] = packed_z

    def panel_halo():
        for y in (0, 16 + DY):
            pack_halo(y, 16)
        for i in range(2):
            strips_z[3 * i, 16 : 16 + DY // 2] = fold_recv[i]
            strips_z[3 * i, 16 + DY // 2 : 16 + DY] = pltpu.roll(fold_recv[i].astype(F32), 64, 1).astype(jnp.bfloat16)
        panel_x((2,))

    def panel_stages(half):
        if half == 0:
            panel_halo()
        yield
        smooth_slope = mm(xpanel[0], wz[:, 256 * half : 256 * half + 256]).astype(jnp.bfloat16)
        zpanel[half, 0] = mm(xpanel[1], wz[:, 256 * half : 256 * half + 128]).astype(jnp.bfloat16)
        zpanel[half, 1] = smooth_slope[:, :128]
        zpanel[half, 2] = smooth_slope[:, 128:]
        yield
        edge_grads = [
            [
                mm(ty[:GY, :WY] if i != 1 else ty[GY:, :WY], zpanel[half, i, WY * side : WY * side + WY]).astype(
                    jnp.bfloat16
                )
                for i in range(3)
            ]
            for side in range(2)
        ]
        yield
        for side in range(2):

            def put(c, p, at=256 * half + 128 * side):
                gpanel[16 * c : 16 * c + 16, at : at + 128] = mm(ay[:, :GY], p).astype(jnp.bfloat16)

            products(lambda i, side=side: edge_grads[side][i], put)
        yield

    def filter_z(z0, g, rows):
        deep, zs, zd = GROUPS[g], zs_all.at[g % 2], zd_all.at[g % 2]
        for y in rows:
            for x in range(0, DX, 128):
                v = [f[z0 + i, y : y + 16, x : x + 128].astype(F32) for i in range(deep + 2 * R)]
                for j in range(deep):
                    c = v[j : j + 7]
                    smooth, slope = c[3] * float(SMOOTH[R]), None
                    for s in (1, 2, 3):
                        smooth = smooth + (c[3 - s] + c[3 + s]) * float(SMOOTH[R + s])
                        term = (c[3 + s] - c[3 - s]) * float(SLOPE[R + s])
                        slope = term if slope is None else slope + term
                    zs[j, y : y + 16, x : x + 128] = smooth.astype(jnp.bfloat16)
                    zd[j, y : y + 16, x : x + 128] = slope.astype(jnp.bfloat16)

    def layer_stages(z0, g, rows=range(0, WY, 16)):
        deep, at_row = GROUPS[g], GY * STARTS[g]
        zs, zd, planes, grads = (ref.at[g % 2] for ref in (zs_all, zd_all, planes_all, grads_all))
        filter_z(z0, g, rows)
        yield
        for j in range(deep):
            pair = mm(ty[:, :WY], zs[j]).astype(jnp.bfloat16)
            at = slice(GY * j, GY * j + GY)
            planes[0, at] = pair[:GY]
            planes[1, at] = pair[GY:]
            planes[2, at] = mm(ty[:GY, :WY], zd[j]).astype(jnp.bfloat16)
        yield
        for i in range(3):
            grads[i, : GY * deep] = mm(planes[i, : GY * deep], xp[:DX] if i == 0 else xp[DX:]).astype(jnp.bfloat16)
        yield
        for y in range(0, GY * deep, 16):

            def put(c, p, y=y):
                prods[c, at_row + y : at_row + y + 16] = p

            products(lambda i, y=y: grads[i, y : y + 16], put)
        yield

    def interleave(*stages):
        for _ in zip(*stages):
            pass

    near_a_z, near_b_z = near_groups(gz)
    ka, kb = GY * GROUPS[0], GY * GROUPS[1]
    rows_first = [(o, c) for o, c in raw if o[0] == 0]
    arrive(rows_first + [(o, c) for o, c in packed if o[0] == 0])
    panel_x((0, 1))
    interleave(layer_stages(near_a_z, 0))
    for c in range(6):
        acc[c] = mm(near_a[:, :ka], prods[c, :ka])

    arrive(raw[:1])
    filter_z(near_b_z, 1, range(16, 16 + DY, 16))
    pack_halo(16, DY)

    arrive([m for group in (packed, raw[1:]) for m in group if m[0][0] == 1])
    interleave(panel_stages(0), layer_stages(near_b_z, 1, (0, 16 + DY)))
    edge_part = mm(gpanel[:, :256], wzx[:256, 128 * QZ :])
    low = lax.broadcasted_iota(jnp.int32, (16, 2 * QX), 1) < QX
    reach = [
        (acc[c, QZ * QY :] + mm(near_b[:, :kb], prods[c, ka : ka + kb])).astype(jnp.bfloat16) for c in range(6)
    ]
    reach = jnp.concatenate([jnp.concatenate(reach[i : i + 2], axis=1) for i in (0, 2, 4)], axis=0)
    reach = mm(reach, mx[:, :128])
    for pair in range(3):
        for q in range(2):
            even, odd = (edge_part[16 * c : 16 * c + 16, 128 * q : 128 * q + 128] for c in (2 * pair, 2 * pair + 1))
            at = 32 * pair + 16 * q
            psend[pair, 16 * q : 16 * q + 16] = (reach[at : at + 16] + jnp.where(low, even, odd)).astype(jnp.bfloat16)
    message((1, 0, 0), psend, precv, [])
    messages[-1][1].start()

    interleave(panel_stages(1), layer_stages(HALF * gz, 2))
    interleave(layer_stages(HALF * gz + GROUPS[2], 3))
    edge_part = mm(gpanel[...], wzx[:, : 128 * QZ])
    for c in range(6):
        s = acc[c, : QZ * QY] + mm(rest[:, : DZ * GY - ka], prods[c, ka:])
        own = mm(s.astype(jnp.bfloat16), mx[:DX, :128])
        for q in range(QZ):
            whole = own[16 * q : 16 * q + 16] + edge_part[16 * c : 16 * c + 16, 128 * q : 128 * q + 128]
            out[c, q] = whole[:, :QX]
    for o, c in messages[:-1]:
        when(o, lambda c=c: c.wait_send())
    messages[-1][1].wait_recv()
    for q in range(2):
        for c in range(6):
            got = precv[c // 2, 16 * q : 16 * q + 16, QX * (c % 2) : QX * (c % 2) + QX].astype(F32)
            out[c, 2 * (1 - gz) + q] += got
    messages[-1][1].wait_send()


def solution(mesh):
    n_row, n_col = mesh.shape["row"], mesh.shape["col"]
    table, places = constants()
    bf = jnp.bfloat16
    hbm = pl.BlockSpec(memory_space=pltpu.HBM)

    def per_device(volume):
        return pl.pallas_call(
            lambda *refs: kernel(n_row, n_col, places, *refs),
            name="structure_tensor",
            out_shape=jax.ShapeDtypeStruct((6, QZ, QY, QX), F32),
            in_specs=[hbm, hbm],
            out_specs=pl.BlockSpec(memory_space=pltpu.VMEM),
            scratch_shapes=[
                pltpu.VMEM((DZ + 2 * R, WY, DX), bf),
                pltpu.VMEM((4, WY, 256), bf),
                pltpu.VMEM((4, WY, 128), bf),
                pltpu.VMEM((2, DY, 128), bf),
                pltpu.VMEM((2, DY // 2, 128), bf),
                pltpu.VMEM((2, DY // 2, 128), bf),
                pltpu.VMEM((2, DEEPEST, WY, DX), bf),
                pltpu.VMEM((2, DEEPEST, WY, DX), bf),
                pltpu.VMEM((2, 3, DEEPEST * GY, DX), bf),
                pltpu.VMEM((2, 3, DEEPEST * GY, DX), bf),
                pltpu.VMEM((6, DZ * GY, DX), bf),
                pltpu.VMEM((6, (QZ + 2) * QY, DX), F32),
                pltpu.VMEM((2, 2 * WY, 384), bf),
                pltpu.VMEM((2, 3, 2 * WY, 128), bf),
                pltpu.VMEM((96, 512), bf),
                pltpu.VMEM((3, 32, 128), bf),
                pltpu.VMEM((3, 32, 128), bf),
                pltpu.VMEM((2 * GY, 256), bf),
                pltpu.VMEM((2 * DX, DX), bf),
                pltpu.VMEM((6 * 16, 512), bf),
                pltpu.VMEM((2 * 16, 256), bf),
                pltpu.VMEM((4 * 16, 1024), bf),
                pltpu.VMEM((2 * DX, 256), bf),
                pltpu.VMEM((256, 256), bf),
                pltpu.VMEM((256, 256), bf),
                pltpu.VMEM((384, 512), bf),
                pltpu.VMEM((16, 256), bf),
                pltpu.VMEM((512, 768), bf),
                pltpu.SemaphoreType.DMA((20,)),
                pltpu.SemaphoreType.DMA((23,)),
                pltpu.SemaphoreType.DMA((23,)),
            ],
            compiler_params=pltpu.CompilerParams(
                collective_id=0, has_side_effects=True, vmem_limit_bytes=VMEM_BYTES
            ),
        )(*[pltpu.with_memory_space_constraint(a, pltpu.HBM) for a in (volume, jnp.asarray(table))])

    return jax.shard_map(
        per_device,
        mesh=mesh,
        in_specs=(P("gz", "row", "col"),),
        out_specs=P(None, "gz", "row", "col"),
        check_vma=False,
    )
```

```python
import itertools

import jax
import jax.numpy as jnp
import ml_dtypes
import numpy as np
from jax import lax
from jax.experimental import pallas as pl
from jax.experimental.pallas import tpu as pltpu
from jax.sharding import PartitionSpec as P

R = 3
R2 = 8
MARGIN = R + R2
BF16 = ml_dtypes.bfloat16
F32 = jnp.float32
MESH = pl.DeviceIdType.MESH

DZ, DY, DX = 16, 64, 256
WY, GY = DY + 32, DY + 2 * R2
QZ, QY, QX = DZ // 4, DY // 4, DX // 4
SLOT = 16
HALF = DZ // 2
GROUPS = (HALF - R, R, HALF // 2, HALF // 2)
STARTS = (0, HALF - R, HALF, HALF + HALF // 2)
DEEPEST = max(GROUPS)
VMEM_BYTES = 32 * 2**20
NEIGHBOURS = tuple(o for o in itertools.product((0, 1), (-1, 0, 1), (-1, 0, 1)) if o != (0, 0, 0))
pair_table = ((0, 0), (1, 1), (2, 2), (0, 1), (0, 2), (1, 2))


def gauss_taps(radius):
    offsets = np.arange(-radius, radius + 1).astype(np.float32)
    spread = np.float32(radius / 3.0)
    smooth = np.exp(-offsets * offsets / (np.float32(2.0) * spread * spread))
    smooth = smooth / np.sum(smooth)
    slopes = offsets * smooth
    slopes = slopes / np.sum(offsets * slopes)
    return [t.astype(BF16).astype(np.float32) for t in (smooth, slopes)]


SMOOTH, SLOPE = gauss_taps(R)
WIDE, _ = gauss_taps(R2)


def banded(taps, radius, source, target):
    s = np.asarray(source)[:, None] - np.asarray(target)[None, :]
    picked = taps[np.clip(s + radius, 0, 2 * radius)]
    return np.where(np.abs(s) <= radius, picked, np.float32(0.0))


def layer_targets(gz):
    return [0, 4, 8, 12] + ([16, 20] if gz == 0 else [-8, -4])


def near_groups(gz):
    return HALF - GROUPS[0] * gz, (DZ - R) * (1 - gz)


def constants():
    y_in, y_out, y_coarse = np.arange(WY) - 16, np.arange(GY) - R2, 4 * np.arange(QY)
    x_all, x_coarse = np.arange(DX), 4 * np.arange(QX)
    ty = []
    for edge in range(3):
        inside = np.ones(GY, np.float32)
        if edge == 0:
            inside[y_out < 0] = 0
        if edge == 2:
            inside[y_out >= DY] = 0
        ty.append(np.concatenate([banded(t, R, y_in, y_out).T * inside[:, None] for t in (SMOOTH, SLOPE)]))
    x_pair = np.stack([banded(SLOPE, R, x_all, x_all), banded(SMOOTH, R, x_all, x_all)])
    ay = banded(WIDE, R2, y_out, y_coarse).T
    near_a, near_b, rest = [], [], []
    for gz in range(2):
        targets = layer_targets(gz)
        a, b = (z0 + np.arange(n) for z0, n in zip(near_groups(gz), GROUPS))
        near_a.append(np.kron(banded(WIDE, R2, a, targets).T, ay))
        near_b.append(np.kron(banded(WIDE, R2, b, targets[QZ:]).T, ay))
        rest_z = np.concatenate([b, HALF * gz + np.arange(HALF)])
        rest.append(np.kron(banded(WIDE, R2, rest_z, targets[:QZ]).T, ay))
    mx = np.zeros((2, DX, 2, QX), np.float32)
    for i in range(2):
        mx[i, R : DX - R, i] = banded(WIDE, R2, x_all[R : DX - R], x_coarse)
    mx = mx.reshape(2 * DX, 2 * QX)
    cols = np.arange(MARGIN)
    pad_in, pad_out = ((0, SLOT - MARGIN), (0, SLOT - MARGIN)), ((0, 0), (0, 0))
    wp = []
    for side_in, x_out, outside in (
        ((cols - MARGIN, cols), cols - R2, lambda x: x < 0),
        ((cols + DX - MARGIN, cols + DX), cols + DX - R, lambda x: x >= DX),
    ):
        for masked in (False, True):
            blocks = []
            for x_in in side_in:
                row = []
                for t in (SMOOTH, SLOPE):
                    w = banded(t, R, x_in, x_out)
                    if masked:
                        w = np.where(outside(x_out)[None, :], np.float32(0.0), w)
                    row.append(np.kron(np.eye(8, dtype=np.float32), np.pad(w, pad_in)))
                blocks.append(np.concatenate(row, axis=1))
            wp.append(np.concatenate(blocks, axis=0))
    wz, wzx = [], []
    one = np.eye(SLOT, dtype=np.float32)
    for gz in range(2):
        z_halo = DZ + np.arange(8) if gz == 0 else np.arange(8) - R
        halves = [HALF * (1 - gz) + np.arange(HALF), HALF * gz + np.arange(HALF)]
        rows = []
        for z_in, used in ((np.arange(DZ), DZ), (z_halo, R)):
            keep = (np.arange(len(z_in)) < used)[:, None]
            rows.append(
                np.concatenate(
                    [np.kron(banded(t, R, z_in, z_out) * keep, one) for z_out in halves for t in (SMOOTH, SLOPE)], axis=1
                )
            )
        wz.append(np.concatenate(rows, axis=0))
        parts = []
        for z_out in halves:
            bz = banded(WIDE, R2, z_out, layer_targets(gz))
            for x_out in (cols - R2, cols + DX - R):
                bx = np.zeros((SLOT, 128), np.float32)
                bx[:MARGIN] = np.tile(banded(WIDE, R2, x_out, x_coarse), 2)
                parts.append(np.kron(bz, bx))
        wzx.append(np.concatenate(parts, axis=0))
    named = {"ty": ty, "xp": [x_pair.reshape(2 * DX, DX)], "near_a": near_a, "near_b": near_b, "rest": rest, "mx": [mx], "wp": wp, "wz": wz, "ay": [ay], "wzx": wzx}
    return pack_table(named)


def pack_table(named):
    blocks, places, at = [], {}, 0
    for name, variants in named.items():
        rows, lanes = variants[0].shape
        cuts = -(-lanes // 256)
        places[name] = (at, rows, cuts)
        for m in variants:
            wide = np.pad(np.asarray(m, np.float32), ((0, 0), (0, 256 * cuts - lanes)))
            blocks += [wide[:, 256 * i : 256 * i + 256] for i in range(cuts)]
            at += rows * cuts
    return np.concatenate(blocks, axis=0).astype(BF16), places


def mm(a, b):
    return jnp.dot(a, b, preferred_element_type=F32)


def kernel(
    n_row, n_col, places,
    vol, table,
    out,
    f, strips, strips_z, send_z, fold_send, fold_recv, zs_all, zd_all, planes_all, grads_all, prods, acc, xpanel, zown, zpanel, gpanel, psend, precv,
    ty, xp, near_a, near_b, rest, mx, wpl, wpr, wz, ay, wzx,
    local_sem, send_sem, recv_sem,
):
    gz, row, col = lax.axis_index("gz"), lax.axis_index("row"), lax.axis_index("col")
    has = {(1, -1): row > 0, (1, 1): row < n_row - 1, (2, -1): col > 0, (2, 1): col < n_col - 1}

    def exists(o):
        tests = [has[d, o[d]] for d in (1, 2) if o[d]]
        if not tests:
            return None
        return tests[0] if len(tests) == 1 else tests[0] & tests[1]

    def when(o, fn):
        ok = exists(o)
        if ok is None:
            fn()
        else:
            pl.when(ok)(fn)

    def peer(o):
        return (lax.rem(gz + o[0], 2), row + o[1], col + o[2])

    barrier = pltpu.get_barrier_semaphore()
    count = 0
    for o in NEIGHBOURS:
        when(o, lambda o=o: pl.semaphore_signal(barrier, inc=1, device_id=peer(o), device_id_type=MESH))
        ok = exists(o)
        count = count + (1 if ok is None else ok.astype(jnp.int32))

    own_z, own_y = pl.ds(R, DZ), pl.ds(16, DY)
    first_y, last_y, top_y, bottom_y = pl.ds(16, 16), pl.ds(DY, 16), pl.ds(0, 16), pl.ds(DY + 16, 16)
    load = pltpu.make_async_copy(vol, f.at[own_z, own_y], local_sem.at[0])
    load.start()
    edge = jnp.where(row == 0, 0, jnp.where(row == n_row - 1, 2, 1))
    fetches = []
    for name, variant, target in (
        ("ty", edge, ty), ("xp", 0, xp), ("near_a", gz, near_a), ("near_b", gz, near_b), ("rest", gz, rest), ("mx", 0, mx),
        ("wp", (col == 0).astype(jnp.int32), wpl), ("wp", 2 + (col == n_col - 1).astype(jnp.int32), wpr),
        ("wz", gz, wz), ("ay", 0, ay), ("wzx", gz, wzx),
    ):
        base, rows, cuts = places[name]
        for i in range(cuts):
            start = pl.multiple_of(base + rows * (cuts * variant + i), 16)
            fetches.append(
                pltpu.make_async_copy(
                    table.at[pl.ds(start, rows)], target.at[:, pl.ds(256 * i, 256)], local_sem.at[1 + len(fetches)]
                )
            )

    near_z = 13 * (1 - gz)
    messages, raw, packed = [], [], []

    def message(o, source, target, group):
        i = len(messages)
        c = pltpu.make_async_remote_copy(
            src_ref=source, dst_ref=target, send_sem=send_sem.at[i], recv_sem=recv_sem.at[i],
            device_id=peer(o), device_id_type=MESH,
        )
        messages.append((o, c))
        group.append((o, c))

    near_layers, halo_layers = pl.ds(near_z, R), pl.ds((R + DZ) * gz, R)
    own_kinds = pl.ds(1, 2)
    y_cut = {0: (pl.ds(0, DY), own_y), 1: (pl.ds(DY - 16, 16), top_y), -1: (pl.ds(0, 16), bottom_y)}
    for o in sorted(NEIGHBOURS, key=lambda o: -(2 * o[0] + abs(o[1]) + abs(o[2])) - 9 * (o == (1, 0, 0))):
        a, b, c = o
        src_y, dst_y = y_cut[b]
        strip_y = pl.ds(16 + (DY - 16 if b == 1 else 0), DY if b == 0 else 16)
        if c == 0 and a == 0:
            message(o, vol.at[:, src_y], f.at[own_z, dst_y], raw)
            message(o, strips.at[own_kinds, strip_y], strips.at[own_kinds, dst_y], packed)
        elif c == 0:
            message(o, vol.at[near_layers, src_y], f.at[halo_layers, dst_y], raw)
        else:
            mine, theirs = (2, 0) if c == 1 else (1, 3)
            if a == 0:
                message(o, strips.at[mine, strip_y], strips.at[theirs, dst_y], packed)
            elif b == 0:
                message(o, fold_send.at[mine - 1], fold_recv.at[theirs // 2], packed)
            else:
                message(o, send_z.at[mine - 1, src_y], strips_z.at[theirs, dst_y], packed)

    for c in fetches:
        c.start()
    dead_z = pl.ds((R + DZ) * gz, R)
    f[dead_z] = jnp.zeros((R, WY, DX), jnp.bfloat16)
    for d, where_y in ((-1, top_y), (1, bottom_y)):
        @pl.when(jnp.logical_not(has[1, d]))
        def _(where_y=where_y):
            f[:, where_y] = jnp.zeros((DZ + 2 * R, 16, DX), jnp.bfloat16)
            strips[:, where_y] = jnp.zeros((4, 16, 256), jnp.bfloat16)
            for kind in (0, 3):
                strips_z[kind, where_y] = jnp.zeros((16, 128), jnp.bfloat16)
    for d, kind in ((-1, 0), (1, 3)):
        @pl.when(jnp.logical_not(has[2, d]))
        def _(kind=kind):
            strips[kind] = jnp.zeros((WY, 256), jnp.bfloat16)
            strips_z[kind] = jnp.zeros((WY, 128), jnp.bfloat16)
            fold_recv[kind // 2] = jnp.zeros((DY // 2, 128), jnp.bfloat16)

    load.wait()

    def pack(layers, y=16, rows=DY):
        lane = lax.broadcasted_iota(jnp.int32, (rows, 128), 1)
        first, last = (jnp.zeros((rows, 128), F32) for _ in range(2))
        for t, z in enumerate(layers):
            tile = f[z, y : y + rows, :]
            use = (lane >= SLOT * t) & (lane < SLOT * t + MARGIN)
            first = jnp.where(use, pltpu.roll(tile[:, :128].astype(F32), SLOT * t, 1), first)
            last = jnp.where(use, pltpu.roll(tile[:, 128:].astype(F32), (SLOT * t + MARGIN) % 128, 1), last)
        return first.astype(jnp.bfloat16), last.astype(jnp.bfloat16)

    for h in range(2):
        first, last = pack([R + HALF * h + t for t in range(8)])
        strips[1, 16 : 16 + DY, 128 * h : 128 * h + 128] = first
        strips[2, 16 : 16 + DY, 128 * h : 128 * h + 128] = last
    for i, packed_z in enumerate(pack([R + near_z + t for t in range(R)])):
        send_z[i] = packed_z
        lower = pltpu.roll(packed_z[DY // 2 :].astype(F32), 64, 1)
        fold_send[i] = (packed_z[: DY // 2].astype(F32) + lower).astype(jnp.bfloat16)

    pl.semaphore_wait(barrier, count)
    for o, c in packed + raw:
        when(o, lambda c=c: c.start())
    for c in fetches:
        c.wait()

    def arrive(group):
        for o, c in group:
            when((o[0], -o[1], -o[2]), lambda c=c: c.wait_recv())

    def products(get, put):
        g = [get(i) for i in range(3)]
        for c, (i, j) in enumerate(pair_table):
            put(c, g[i] * g[j])

    panel_sides = ((0, wpl), (2, wpr))

    def panel_x(tiles):
        for side, (k, w) in enumerate(panel_sides):
            rows = []
            for t in tiles:
                src = [(strips[i, :, 128 * t : 128 * t + 128] if t < 2 else strips_z[i]) for i in (k, k + 1)]
                rows.append(jnp.concatenate(src, axis=1))
            xs = mm(jnp.concatenate(rows, axis=0), w[...]).astype(jnp.bfloat16)
            for i, t in enumerate(tiles):
                piece = xs[WY * i : WY * i + WY]
                xpanel[0, WY * side : WY * side + WY, 128 * t : 128 * t + 128] = piece[:, :128]
                xpanel[1, WY * side : WY * side + WY, 128 * t : 128 * t + 128] = piece[:, 128:]

    def pack_halo(y, rows):
        halo_z = (R + DZ) * (1 - gz)
        for i, packed_z in enumerate(pack([halo_z + t for t in range(R)], y, rows)):
            strips_z[1 + i, y : y + rows] = packed_z

    def panel_halo():
        for y in (0, 16 + DY):
            pack_halo(y, 16)
        for i in range(2):
            strips_z[3 * i, 16 : 16 + DY // 2] = fold_recv[i]
            strips_z[3 * i, 16 + DY // 2 : 16 + DY] = pltpu.roll(fold_recv[i].astype(F32), 64, 1).astype(jnp.bfloat16)
        panel_x((2,))

    def panel_stages(half):
        if half == 0:
            panel_halo()
        yield
        if half == 0:
            halo_part = [mm(xpanel[i, :, 256:], wz[256:, : 256 - 128 * i]) for i in range(2)]
            smooth_slope = (zown[:, :256] + halo_part[0]).astype(jnp.bfloat16)
            zpanel[half, 0] = (zown[:, 256:] + halo_part[1]).astype(jnp.bfloat16)
        else:
            smooth_slope = mm(xpanel[0], wz[:, 256:]).astype(jnp.bfloat16)
            zpanel[half, 0] = mm(xpanel[1], wz[:, 256:384]).astype(jnp.bfloat16)
        zpanel[half, 1] = smooth_slope[:, :128]
        zpanel[half, 2] = smooth_slope[:, 128:]
        yield
        edge_grads = [
            [
                mm(ty[:GY, :WY] if i != 1 else ty[GY:, :WY], zpanel[half, i, WY * side : WY * side + WY]).astype(
                    jnp.bfloat16
                )
                for i in range(3)
            ]
            for side in range(2)
        ]
        yield
        for side in range(2):

            def put(c, p, at=256 * half + 128 * side):
                gpanel[16 * c : 16 * c + 16, at : at + 128] = mm(ay[:, :GY], p).astype(jnp.bfloat16)

            products(lambda i, side=side: edge_grads[side][i], put)
        yield

    def filter_z(z0, g, rows):
        deep, zs, zd = GROUPS[g], zs_all.at[g % 2], zd_all.at[g % 2]
        for y in rows:
            for x in range(0, DX, 128):
                v = [f[z0 + i, y : y + 16, x : x + 128].astype(F32) for i in range(deep + 2 * R)]
                for j in range(deep):
                    c = v[j : j + 7]
                    smooth, slope = c[3] * float(SMOOTH[R]), None
                    for s in (1, 2, 3):
                        smooth = smooth + (c[3 - s] + c[3 + s]) * float(SMOOTH[R + s])
                        term = (c[3 + s] - c[3 - s]) * float(SLOPE[R + s])
                        slope = term if slope is None else slope + term
                    zs[j, y : y + 16, x : x + 128] = smooth.astype(jnp.bfloat16)
                    zd[j, y : y + 16, x : x + 128] = slope.astype(jnp.bfloat16)

    def layer_stages(z0, g, rows=range(0, WY, 16)):
        deep, at_row = GROUPS[g], GY * STARTS[g]
        zs, zd, planes, grads = (ref.at[g % 2] for ref in (zs_all, zd_all, planes_all, grads_all))
        filter_z(z0, g, rows)
        yield
        for j in range(deep):
            pair = mm(ty[:, :WY], zs[j]).astype(jnp.bfloat16)
            at = slice(GY * j, GY * j + GY)
            planes[0, at] = pair[:GY]
            planes[1, at] = pair[GY:]
            planes[2, at] = mm(ty[:GY, :WY], zd[j]).astype(jnp.bfloat16)
        yield
        for i in range(3):
            grads[i, : GY * deep] = mm(planes[i, : GY * deep], xp[:DX] if i == 0 else xp[DX:]).astype(jnp.bfloat16)
        yield
        for y in range(0, GY * deep, 16):

            def put(c, p, y=y):
                prods[c, at_row + y : at_row + y + 16] = p

            products(lambda i, y=y: grads[i, y : y + 16], put)
        yield

    def interleave(*stages):
        for _ in zip(*stages):
            pass

    near_a_z, near_b_z = near_groups(gz)
    ka, kb = GY * GROUPS[0], GY * GROUPS[1]
    rows_first = [(o, c) for o, c in raw if o[0] == 0]
    arrive(rows_first + [(o, c) for o, c in packed if o[0] == 0])
    panel_x((0, 1))
    for i in range(2):
        zown[:, 256 * i : 256 + 128 * i] = mm(xpanel[i, :, :256], wz[:256, : 256 - 128 * i])
    interleave(layer_stages(near_a_z, 0))
    for c in range(6):
        acc[c] = mm(near_a[:, :ka], prods[c, :ka])

    arrive(raw[:1])
    filter_z(near_b_z, 1, range(16, 16 + DY, 16))
    pack_halo(16, DY)

    arrive([m for group in (packed, raw[1:]) for m in group if m[0][0] == 1])
    interleave(panel_stages(0), layer_stages(near_b_z, 1, (0, 16 + DY)))
    edge_part = mm(gpanel[:, :256], wzx[:256, 128 * QZ :])
    low = lax.broadcasted_iota(jnp.int32, (16, 2 * QX), 1) < QX
    reach = [
        (acc[c, QZ * QY :] + mm(near_b[:, :kb], prods[c, ka : ka + kb])).astype(jnp.bfloat16) for c in range(6)
    ]
    reach = jnp.concatenate([jnp.concatenate(reach[i : i + 2], axis=1) for i in (0, 2, 4)], axis=0)
    reach = mm(reach, mx[:, :128])
    for pair in range(3):
        for q in range(2):
            even, odd = (edge_part[16 * c : 16 * c + 16, 128 * q : 128 * q + 128] for c in (2 * pair, 2 * pair + 1))
            at = 32 * pair + 16 * q
            psend[pair, 16 * q : 16 * q + 16] = (reach[at : at + 16] + jnp.where(low, even, odd)).astype(jnp.bfloat16)
    message((1, 0, 0), psend, precv, [])
    messages[-1][1].start()

    interleave(panel_stages(1), layer_stages(HALF * gz, 2))
    interleave(layer_stages(HALF * gz + GROUPS[2], 3))
    edge_part = mm(gpanel[...], wzx[:, : 128 * QZ])
    for c in range(6):
        s = acc[c, : QZ * QY] + mm(rest[:, : DZ * GY - ka], prods[c, ka:])
        own = mm(s.astype(jnp.bfloat16), mx[:DX, :128])
        for q in range(QZ):
            whole = own[16 * q : 16 * q + 16] + edge_part[16 * c : 16 * c + 16, 128 * q : 128 * q + 128]
            out[c, q] = whole[:, :QX]
    for o, c in messages[:-1]:
        when(o, lambda c=c: c.wait_send())
    messages[-1][1].wait_recv()
    for q in range(2):
        for c in range(6):
            got = precv[c // 2, 16 * q : 16 * q + 16, QX * (c % 2) : QX * (c % 2) + QX].astype(F32)
            out[c, 2 * (1 - gz) + q] += got
    messages[-1][1].wait_send()


def solution(mesh):
    n_row, n_col = mesh.shape["row"], mesh.shape["col"]
    table, places = constants()
    bf = jnp.bfloat16
    hbm = pl.BlockSpec(memory_space=pltpu.HBM)

    def per_device(volume):
        return pl.pallas_call(
            lambda *refs: kernel(n_row, n_col, places, *refs),
            name="structure_tensor",
            out_shape=jax.ShapeDtypeStruct((6, QZ, QY, QX), F32),
            in_specs=[hbm, hbm],
            out_specs=pl.BlockSpec(memory_space=pltpu.VMEM),
            scratch_shapes=[
                pltpu.VMEM((DZ + 2 * R, WY, DX), bf),
                pltpu.VMEM((4, WY, 256), bf),
                pltpu.VMEM((4, WY, 128), bf),
                pltpu.VMEM((2, DY, 128), bf),
                pltpu.VMEM((2, DY // 2, 128), bf),
                pltpu.VMEM((2, DY // 2, 128), bf),
                pltpu.VMEM((2, DEEPEST, WY, DX), bf),
                pltpu.VMEM((2, DEEPEST, WY, DX), bf),
                pltpu.VMEM((2, 3, DEEPEST * GY, DX), bf),
                pltpu.VMEM((2, 3, DEEPEST * GY, DX), bf),
                pltpu.VMEM((6, DZ * GY, DX), bf),
                pltpu.VMEM((6, (QZ + 2) * QY, DX), F32),
                pltpu.VMEM((2, 2 * WY, 384), bf),
                pltpu.VMEM((2 * WY, 384), F32),
                pltpu.VMEM((2, 3, 2 * WY, 128), bf),
                pltpu.VMEM((96, 512), bf),
                pltpu.VMEM((3, 32, 128), bf),
                pltpu.VMEM((3, 32, 128), bf),
                pltpu.VMEM((2 * GY, 256), bf),
                pltpu.VMEM((2 * DX, DX), bf),
                pltpu.VMEM((6 * 16, 512), bf),
                pltpu.VMEM((2 * 16, 256), bf),
                pltpu.VMEM((4 * 16, 1024), bf),
                pltpu.VMEM((2 * DX, 256), bf),
                pltpu.VMEM((256, 256), bf),
                pltpu.VMEM((256, 256), bf),
                pltpu.VMEM((384, 512), bf),
                pltpu.VMEM((16, 256), bf),
                pltpu.VMEM((512, 768), bf),
                pltpu.SemaphoreType.DMA((20,)),
                pltpu.SemaphoreType.DMA((23,)),
                pltpu.SemaphoreType.DMA((23,)),
            ],
            compiler_params=pltpu.CompilerParams(
                collective_id=0, has_side_effects=True, vmem_limit_bytes=VMEM_BYTES
            ),
        )(*[pltpu.with_memory_space_constraint(a, pltpu.HBM) for a in (volume, jnp.asarray(table))])

    return jax.shard_map(
        per_device,
        mesh=mesh,
        in_specs=(P("gz", "row", "col"),),
        out_specs=P(None, "gz", "row", "col"),
        check_vma=False,
    )
```
